32 devices in a mesh: rep: 4 (over y, core), fsdp: 8 (over z, x).
Axes of the slice: x: 2, y: 2, z: 4, core: 2. Of those that a mesh axis runs over, the one named last changes fastest.
Arguments:
- hidden: bfloat16 [24576, 768], P(('rep', 'fsdp')), may hold values from -6 to 6
- cotangent: bfloat16 [24576, 768], P(('rep', 'fsdp')), may hold values from -6 to 6
- lengths: int32 [192], P(('rep', 'fsdp')), may hold values from 16 to 128, as said below
- bounds: int32 [192], P(('rep', 'fsdp')), may hold values from 1 to 127, as said below
- timesteps: int32 [192], P(('rep', 'fsdp')), may hold values from 0 to 1999
- weight_qkv: bfloat16 [768, 2304], P('fsdp'), may hold values from -0.21875 to 0.21875
- bias_qv: bfloat16 [1536], P('fsdp'), may hold values from -3 to 3
- weight_out: bfloat16 [768, 768], P('fsdp'), may hold values from -0.625 to 0.625
- bias_out: bfloat16 [768], P('fsdp'), may hold values from -3 to 3
- gain_mid: bfloat16 [768], P('fsdp'), may hold values from 0.099609375 to 1.8984375
- shift_mid: bfloat16 [768], P('fsdp'), may hold values from -3 to 3
- weight_up: bfloat16 [768, 3072], P('fsdp'), may hold values from -0.21875 to 0.21875
- bias_up: bfloat16 [3072], P('fsdp'), may hold values from -3 to 3
- weight_down: bfloat16 [3072, 768], P('fsdp'), may hold values from -0.109375 to 0.109375
- bias_down: bfloat16 [768], P('fsdp'), may hold values from -3 to 3
- gain_last: bfloat16 [768], P('fsdp'), may hold values from 0.099609375 to 1.8984375
- shift_last: bfloat16 [768], P('fsdp'), may hold values from -3 to 3
- weight_time: bfloat16 [768, 128], P('fsdp'), may hold values from -0.5 to 0.5
Outputs:
- activations: bfloat16 [24576, 768], P(('rep', 'fsdp'))
- grad_hidden: bfloat16 [24576, 768], P(('rep', 'fsdp'))
- grad_weight_qkv: float32 [768, 2304], P('fsdp')
- grad_bias_qv: float32 [1536], P('fsdp')
- grad_weight_out: float32 [768, 768], P('fsdp')
- grad_bias_out: float32 [768], P('fsdp')
- grad_gain_mid: float32 [768], P('fsdp')
- grad_shift_mid: float32 [768], P('fsdp')
- grad_weight_up: float32 [768, 3072], P('fsdp')
- grad_bias_up: float32 [3072], P('fsdp')
- grad_weight_down: float32 [3072, 768], P('fsdp')
- grad_bias_down: float32 [768], P('fsdp')
- grad_gain_last: float32 [768], P('fsdp')
- grad_shift_last: float32 [768], P('fsdp')
- grad_weight_time: float32 [768, 128], P('fsdp')
The draws below stay inside these ranges and needn't reach their ends.
Inputs may be any that keep to these rules, and one draw needn't show every extreme that they name: `lengths`: the first of each device's 6 sequences (every 6-th from 0) has length 128; sequence 1 has length 16. `bounds`: each boundary is at least 1 and below its sequence's length; sequence 0 has boundary 128 - 1 and sequence 1 has boundary 1.
All inputs are finite; a program needn't handle non-finite values.
Results may differ from the reference program's by a relative error of at most 0.019.
Values may be sent and summed in bfloat16 or wider, within the bound.
No kernel may reach another device: no remote copies, remote signals or barrier semaphores. Data moves between devices by JAX's collectives and lax.ppermute only.
A program may use at most 192 MiB of HBM per device.

```python
import math
import jax
import jax.numpy as jnp
from jax import lax

D = 768
HEADS = 12
HEAD_DIM = 64
FF = 3072
TFREQ = 128
TSTEPS = 2000
SEQ = 128
SEQ_DEV = 6
SEQS = 192
TOKENS = 24576


def shared_lengths(key):
    inner = jax.random.fold_in(key, 11)
    base = jax.random.randint(inner, (SEQS,), SEQ // 8, SEQ + 1)
    places = jnp.arange(SEQS)
    first = places % SEQ_DEV == 0
    lengths = jnp.where(first, SEQ, base)
    lengths = jnp.where(places == 1, SEQ // 8, lengths)
    return lengths.astype(jnp.int32)


def draw_lengths(key, part):
    return shared_lengths(key)


def draw_bounds(key, part):
    lengths = shared_lengths(key)
    key = jax.random.fold_in(key, 2)
    bounds = jax.random.randint(key, (SEQS,), 1, lengths)
    places = jnp.arange(SEQS)
    bounds = jnp.where(places == 0, SEQ - 1, bounds)
    bounds = jnp.where(places == 1, 1, bounds)
    return bounds.astype(jnp.int32)


def set_ends(entries, stream_key, smallest, top_value):
    shape = entries.shape
    index_at = [jax.random.randint(jax.random.fold_in(stream_key, axis), (), 0, shape[axis]) for axis in range(len(shape))]
    entries = entries.at[tuple(index_at)].set(smallest)
    longest = shape.index(max(shape))
    index_at[longest] = (index_at[longest] + 1) % shape[longest]
    return entries.at[tuple(index_at)].set(top_value)


def shard_levels(stream_key, extent, cuts, smallest, top_value):
    def one(dim, parts):
        steps = jax.random.uniform(jax.random.fold_in(jax.random.fold_in(stream_key, 6), dim), (parts,), jnp.float32, smallest / len(cuts), top_value / len(cuts))
        return jnp.repeat(jnp.exp(steps), extent[dim] // parts).reshape((-1,) + (1,) * (len(extent) - dim - 1))

    loudness = one(*cuts[0])
    for cut in cuts[1:]:
        loudness = loudness * one(*cut)
    return loudness


def noise(rng, extent, width, bound, split=(), held_as=jnp.bfloat16):
    values = width * jax.random.normal(rng, extent, jnp.float32)
    if split:
        values = values * shard_levels(rng, extent, split, -0.22, 0.18)
    return jnp.clip(values, -bound, bound).astype(held_as)


def setup_inputs(seed: int = 0) -> dict:
    seeds = jax.random.split(jax.random.key(seed), 19)
    hidden = noise(seeds[0], (TOKENS, D), 1.0, 6.0, ((0, 32),))
    cotangent = noise(seeds[1], (TOKENS, D), 1.0, 6.0, ((0, 32),))
    lengths = draw_lengths(jax.random.fold_in(seeds[18], 71), 0)
    bounds = draw_bounds(jax.random.fold_in(seeds[18], 71), 0)
    timesteps = set_ends(jax.random.randint(seeds[4], (SEQS,), 0, TSTEPS), jax.random.fold_in(seeds[4], 1), 0, TSTEPS - 1).astype(jnp.int32)
    weight_qkv = noise(seeds[5], (D, 3 * D), D ** -0.5, 0.21875, ((0, 8),))
    bias_qv = noise(seeds[6], (2 * D,), 0.5, 3.0, ((0, 8),))
    weight_out = noise(seeds[7], (D, D), (D // 8) ** -0.5, 0.625, ((0, 8),))
    bias_out = noise(seeds[8], (D,), 0.5, 3.0, ((0, 8),))
    gain_mid = jnp.clip(1.0 + 0.18 * jax.random.normal(seeds[9], (D,), jnp.float32), 0.099609375, 1.8984375).astype(jnp.bfloat16)
    shift_mid = noise(seeds[10], (D,), 0.5, 3.0, ((0, 8),))
    weight_up = noise(seeds[11], (D, FF), D ** -0.5, 0.21875, ((0, 8),))
    bias_up = noise(seeds[12], (FF,), 0.5, 3.0, ((0, 8),))
    weight_down = noise(seeds[13], (FF, D), FF ** -0.5, 0.109375, ((0, 8),))
    bias_down = noise(seeds[14], (D,), 0.5, 3.0, ((0, 8),))
    gain_last = jnp.clip(1.0 + 0.18 * jax.random.normal(seeds[15], (D,), jnp.float32), 0.099609375, 1.8984375).astype(jnp.bfloat16)
    shift_last = noise(seeds[16], (D,), 0.5, 3.0, ((0, 8),))
    weight_time = noise(seeds[17], (D, TFREQ), TFREQ ** -0.5, 0.5, ((0, 8),))
    return dict(hidden=hidden, cotangent=cotangent, lengths=lengths, bounds=bounds, timesteps=timesteps, weight_qkv=weight_qkv, bias_qv=bias_qv, weight_out=weight_out, bias_out=bias_out, gain_mid=gain_mid, shift_mid=shift_mid, weight_up=weight_up, bias_up=bias_up, weight_down=weight_down, bias_down=bias_down, gain_last=gain_last, shift_last=shift_last, weight_time=weight_time)


@jax.custom_vjp
def low(v):
    return lax.optimization_barrier(v.astype(jnp.bfloat16)).astype(jnp.float32)

@jax.custom_vjp
def low_back(v):
    return v

def low_keep(v):
    return (low(v), None)

def low_pass(kept, grad):
    return (grad,)

def back_keep(v):
    return (v, None)

def back_low(kept, grad):
    return (low(grad),)
low.defvjp(low_keep, low_pass)
low_back.defvjp(back_keep, back_low)

def time_features(timesteps):
    half = TFREQ // 2
    freqs = jnp.exp(-math.log(10000.0) * jnp.arange(half).astype(jnp.float32) / half)
    angles = timesteps.astype(jnp.float32)[:, None] * freqs[None, :]
    return jnp.concatenate([jnp.cos(angles), jnp.sin(angles)], axis=1)

def layer_norm(value, gain, shift):
    mean = lax.optimization_barrier(jnp.mean(value, -1, keepdims=True))
    centered = value - mean
    variance = lax.optimization_barrier(jnp.mean(centered * centered, -1, keepdims=True))
    return centered * lax.rsqrt(variance + 1e-05) * gain + shift

def forward(rows, params, feats, target, valid):
    weight_qkv, bias_qv, weight_out, bias_out, gain_mid, shift_mid, weight_up, bias_up, weight_down, bias_down, gain_last, shift_last, weight_time = params
    highest = lax.Precision.HIGHEST
    group = feats.shape[0]
    temb = jnp.dot(low(feats), weight_time.T, precision=highest)
    start = rows.reshape(group, SEQ, D) + target[:, :, None] * temb[:, None, :]
    start_low = low(start)
    proj = jnp.einsum('gsd,de->gse', start_low, weight_qkv, precision=highest)
    query = low(low_back((proj[..., :D] + bias_qv[:D]) * HEAD_DIM ** (-0.5)))
    key = low(low_back(proj[..., D:2 * D]))
    value = low(low_back(proj[..., 2 * D:] + bias_qv[D:]))
    query = query.reshape(group, SEQ, HEADS, HEAD_DIM)
    key = key.reshape(group, SEQ, HEADS, HEAD_DIM)
    value = value.reshape(group, SEQ, HEADS, HEAD_DIM)
    scores = low_back(jnp.einsum('gqhe,gkhe->ghqk', query, key, precision=highest))
    scores = jnp.where(valid[:, None, None, :] > 0, scores, -1e+30)
    top = lax.optimization_barrier(jnp.max(scores, -1, keepdims=True))
    expo = jnp.exp(scores - top)
    probs = low(expo / lax.optimization_barrier(jnp.sum(expo, -1, keepdims=True)))
    mixed = jnp.einsum('ghqk,gkhe->gqhe', probs, value, precision=highest).reshape(group, SEQ, D)
    mixed = low(low_back(mixed))
    branch = low_back(jnp.einsum('gsd,de->gse', mixed, weight_out, precision=highest) + bias_out)
    middle = layer_norm(start + branch, gain_mid, shift_mid)
    upward = low_back(jnp.einsum('gsd,df->gsf', low(middle), weight_up, precision=highest) + bias_up)
    acted = low(jax.nn.gelu(upward))
    downward = low_back(jnp.einsum('gsf,fd->gsd', acted, weight_down, precision=highest) + bias_down)
    result = layer_norm(middle + downward, gain_last, shift_last) * valid[:, :, None]
    return result.reshape(group * SEQ, D)

def reference(hidden, cotangent, lengths, bounds, timesteps, weight_qkv, bias_qv, weight_out, bias_out, gain_mid, shift_mid, weight_up, bias_up, weight_down, bias_down, gain_last, shift_last, weight_time):
    params = tuple((item.astype(jnp.float32) for item in (weight_qkv, bias_qv, weight_out, bias_out, gain_mid, shift_mid, weight_up, bias_up, weight_down, bias_down, gain_last, shift_last, weight_time)))
    group = math.gcd(SEQS, 32)
    count = SEQS // group
    places = jnp.arange(SEQ).astype(jnp.int32)
    valid = (places[None, :] < lengths[:, None]).astype(jnp.float32)
    target = (places[None, :] >= bounds[:, None]).astype(jnp.float32)
    feats = time_features(timesteps)
    items = (hidden.astype(jnp.float32).reshape(count, group * SEQ, D), cotangent.astype(jnp.float32).reshape(count, group * SEQ, D), feats.reshape(count, group, TFREQ), target.reshape(count, group, SEQ), valid.reshape(count, group, SEQ))

    def one_group(carry, item):
        rows_g, cot_g, feats_g, target_g, valid_g = item
        result, pull = jax.vjp(lambda rows, weights: forward(rows, weights, feats_g, target_g, valid_g), rows_g, params)
        grad_rows, grad_params = pull(cot_g)
        carry = tuple((total + part for total, part in zip(carry, grad_params)))
        return (carry, (result.astype(jnp.bfloat16), grad_rows.astype(jnp.bfloat16)))
    init = tuple((jnp.zeros_like(item) for item in params))
    grads, (outputs, grad_rows) = lax.scan(one_group, init, items)
    return (outputs.reshape(TOKENS, D), grad_rows.reshape(TOKENS, D), grads[0], grads[1], grads[2], grads[3], grads[4], grads[5], grads[6], grads[7], grads[8], grads[9], grads[10], grads[11], grads[12])
```

```python
import functools
import math

import jax
import jax.numpy as jnp
from jax import lax
from jax.experimental import pallas as pl
from jax.experimental.pallas import tpu as pltpu
from jax.sharding import PartitionSpec as P

HEADS = 12
TFREQ = 128
XS = 2
TALL = 16
WIDE = jnp.float32
HALF = jnp.bfloat16
MIB = 1024 * 1024
(BIAS_Q, BIAS_V, BIAS_OUT, GAIN_MID, SHIFT_MID, BIAS_UP, BIAS_DOWN, GAIN_LAST, SHIFT_LAST) = (0, 1, 2, 3, 4, 5, 9, 10, 11)

ANYWHERE = pl.BlockSpec(memory_space=pltpu.HBM)
SCALARS = pl.BlockSpec(memory_space=pltpu.SMEM)


def dot(left, right, axes=(1, 0)):
    return lax.dot_general(
        left, right, (((axes[0],), (axes[1],)), ((), ())), preferred_element_type=WIDE
    )


def shape(dims, dtype=HALF):
    return jax.ShapeDtypeStruct(tuple(dims), dtype)


def held(dims, dtype=HALF):
    return pltpu.VMEM(tuple(dims), dtype)


def near(*values):
    return [pltpu.with_memory_space_constraint(v, pltpu.VMEM) for v in values]


def far(*values):
    return [pltpu.with_memory_space_constraint(v, pltpu.HBM) for v in values]


def fixed(dims):
    return pl.BlockSpec(tuple(dims), lambda *_: (0,) * len(dims))


def call(kernel, grid, in_specs, out_specs, out_shape, scratch=(), prefetch=(), after=(), aliases=None, flops=0, vmem=24, cost=1.0):
    after = list(after)
    count, n = len(in_specs), len(after)

    def run(*refs):
        start = len(prefetch) + count
        kernel(*refs[:start], *refs[start + n :])

    return lambda *operands: pl.pallas_call(
        run,
        grid_spec=pltpu.PrefetchScalarGridSpec(
            num_scalar_prefetch=len(prefetch),
            grid=grid,
            in_specs=in_specs + [ANYWHERE] * n,
            out_specs=out_specs,
            scratch_shapes=list(scratch),
        ),
        out_shape=out_shape,
        input_output_aliases=aliases or {},
        compiler_params=pltpu.CompilerParams(vmem_limit_bytes=vmem * MIB),
        cost_estimate=pl.CostEstimate(flops=int(cost * 0.25e9), bytes_accessed=int(cost * 0.25e6), transcendentals=0),
    )(*prefetch, *operands, *after)


def norm_parts(value):
    mean = jnp.mean(value, -1, keepdims=True)
    centered = value - mean
    inverse = lax.rsqrt(jnp.mean(centered * centered, -1, keepdims=True) + 1e-05)
    return centered * inverse, inverse


def norm_back(grad, normed, inverse):
    return inverse * (
        grad
        - jnp.mean(grad, -1, keepdims=True)
        - normed * jnp.mean(grad * normed, -1, keepdims=True)
    )


def flip(index, by):
    return 1 - index if by else index


class Gathered:
    def __init__(self, arrays, segments, dims):
        self.arrays, self.segments, self.dims = list(arrays), list(segments), tuple(dims)
        self.zs = dims[0]

    def load(self, refs, place, target, sem):
        zs, _, _, rows, columns = self.dims
        z0, x0, y0, c0 = (place[i] for i in range(4))
        wide = columns // 2
        cut = self.arrays[0].shape[0]
        for n, low, count, dz, dx, dy, dc, column in self.segments:
            z = lax.rem(z0 + (zs - dz), zs)
            while count:
                block = column // wide
                step = min(count, (block + 1) * wide - column)
                first = pl.multiple_of(flip(c0, dc) * wide + column % wide, 128)
                there = target.at[
                    z, flip(x0, dx), flip(y0, dy), pl.ds(block * cut, cut), pl.ds(first, step)
                ]
                pltpu.make_async_copy(refs[n].at[:, pl.ds(low, step)], there, sem).start()
                low, column, count = low + step, column + step, count - step
        pltpu.make_async_copy(target, target, sem).wait()


class Whole:
    def __init__(self, array):
        self.arrays, self.dims = [array], array.shape

    def load(self, refs, place, target, sem):
        copy = pltpu.make_async_copy(refs[0], target, sem)
        copy.start()
        copy.wait()


def load(copies):
    for copy in copies:
        copy.start()
    for copy in copies:
        copy.wait()


def columns_of(ref, low, high):
    value = ref[..., low:high]
    return value.reshape(-1, high - low)


def whole_specs(values):
    return [fixed(v.shape) for v in values]


def vector_map(shards):
    index = lax.broadcasted_iota(jnp.int32, (TALL * shards, 1), 0)
    shard, r = index // TALL, index % TALL
    half, quarter = shards // 2, shards // 4
    query, up = r < 2, (r >= BIAS_UP) & (r < BIAS_DOWN)
    kinds = jnp.where(query, shard // half, jnp.where(up, BIAS_UP + shard // quarter, r))
    spots = jnp.where(
        query, 2 * (shard % half) + r, jnp.where(up, 4 * (shard % quarter) + r - BIAS_UP, shard)
    )
    return kinds, spots


def selector(width, shards):
    each = width // shards
    row = lax.broadcasted_iota(jnp.int32, (width, shards * TFREQ), 0)
    column = lax.broadcasted_iota(jnp.int32, (width, shards * TFREQ), 1)
    lane = column % TFREQ
    return ((row == (column // TFREQ) * each + lane) & (lane < each)).astype(HALF)


def kind_rows(kinds, shards):
    return (kinds == lax.broadcasted_iota(jnp.int32, (TALL * shards, TALL), 1)).astype(HALF)


def table_of(pieces, width, shards):
    kinds, spots = vector_map(shards)
    wide = jnp.concatenate([jnp.where(spots == m, pieces, jnp.zeros_like(pieces)) for m in range(shards)], axis=1)
    spread = dot(wide, selector(width, shards), (1, 1)).astype(HALF)
    return dot(kind_rows(kinds, shards), spread, (0, 0))


def pieces_of(table, width, shards):
    kinds, spots = vector_map(shards)
    spread = dot(dot(kind_rows(kinds, shards), table).astype(HALF), selector(width, shards))
    out = jnp.zeros((TALL * shards, TFREQ), WIDE)
    for m in range(shards):
        out = jnp.where(spots == m, spread[:, m * TFREQ : (m + 1) * TFREQ], out)
    return out.astype(HALF)


def add_time(start_of, bounds_ref, temb, seqs, span, use):
    places = lax.broadcasted_iota(jnp.int32, (span, 1), 0)
    for s in range(seqs):
        at = slice(s * span, (s + 1) * span)
        target = jnp.where(places >= bounds_ref[s], 1.0, 0.0)
        use(at, start_of[at, :].astype(WIDE) + target * temb[s : s + 1, :])


def project(place, bounds, hidden, feats, group, known, dims, after=()):
    rows, width, seqs = dims
    span = rows // seqs
    half = 3 * width // 2
    scale = (width // HEADS) ** (-0.5)
    n = len(group.arrays)
    wide = half + TFREQ

    def kernel(place_ref, bounds_ref, hidden_ref, feats_ref, *refs):
        ins, refs = refs[:n], refs[n:]
        if known:
            time_in, vec_in = refs[:2]
            refs = refs[2:]
        start_ref, qkv_ref, vec_ref, time_ref, w_ref, sem = refs
        group.load(ins, place_ref, w_ref, sem)
        if known:
            time_ref[...], table = time_in[...], vec_in[...]
        else:
            time_ref[...] = columns_of(w_ref, half, wide)
            shards = group.zs * XS
            pieces = columns_of(w_ref, wide + half, 2 * wide).reshape(shards, width // shards, TFREQ)
            table = table_of(pieces[:, :TALL].reshape(shards * TALL, TFREQ), width, shards)
        vec_ref[...] = table
        temb = dot(feats_ref[...], time_ref[...], (1, 1))

        def use(at, start):
            start_ref[at, :] = start.astype(HALF)

        add_time(hidden_ref, bounds_ref, temb, seqs, span, use)
        start_b = start_ref[...]
        first = dot(start_b, columns_of(w_ref, 0, half))
        qkv_ref[:, :width] = ((first[:, :width] + table[BIAS_Q : BIAS_Q + 1]) * scale).astype(HALF)
        qkv_ref[:, width:half] = first[:, width:].astype(HALF)
        second = dot(start_b, columns_of(w_ref, wide, wide + half))
        rest = half - width
        qkv_ref[:, half : half + rest] = second[:, :rest].astype(HALF)
        qkv_ref[:, 2 * width :] = (second[:, rest:] + table[BIAS_V : BIAS_V + 1]).astype(HALF)

    extra = list(known) if known else []
    outs = [held((rows, width)), held((rows, 3 * width)), held((TALL, width), WIDE), held((width, TFREQ)), held(group.dims)]
    return call(
        kernel,
        (1,),
        [SCALARS, SCALARS] + whole_specs([hidden, feats]) + [ANYWHERE] * n + whole_specs(extra),
        whole_specs(outs),
        outs,
        [pltpu.SemaphoreType.DMA],
        after=after,
        flops=rows * width * width * 6,
        cost=7, vmem=6,
    )(place, bounds, hidden, feats, *far(*group.arrays), *extra)


def attend(lens, qkv, dims, after=()):
    rows, width, seqs = dims
    span = rows // seqs
    pairs = width // 128

    def kernel(lens_ref, qkv_ref, mixed_ref, stats_ref):
        lane = lax.broadcasted_iota(jnp.int32, (span, 128), 1)
        low = lane < 64

        @pl.loop(0, seqs)
        def _(s):
            at = pl.ds(pl.multiple_of(s * span, span), span)
            keep = lane < lens_ref[s]
            stats = jnp.zeros((span, 128), WIDE)
            for p in range(pairs):
                cols = lambda m: slice(m * width + p * 128, m * width + (p + 1) * 128)
                keys = pair_split(qkv_ref[at, cols(1)], low)
                values = pair_split(qkv_ref[at, cols(2)], low)
                scores = dot(qkv_ref[at, cols(0)], keys, (1, 1))
                probs = []
                for h in range(2):
                    one = jnp.where(keep, scores[:, h * span : (h + 1) * span], -1e30)
                    top = jnp.max(one, -1, keepdims=True)
                    expo = jnp.exp(one - top)
                    total = jnp.sum(expo, -1, keepdims=True)
                    probs.append((expo * (1.0 / total)).astype(HALF))
                    stats = jnp.where(lane == 2 * p + h, top + jnp.log(total), stats)
                mixed_ref[at, cols(0)] = dot(jnp.concatenate(probs, axis=1), values).astype(HALF)
            stats_ref[at, :] = stats

    outs = [held((rows, width)), held((rows, 128), WIDE)]
    return call(
        kernel,
        (1,),
        [SCALARS] + whole_specs([qkv]),
        whole_specs(outs),
        outs,
        after=after,
        flops=rows * width * width * 6,
        cost=7, vmem=4,
    )(lens, *near(qkv))


def raise_up(place, bounds, hidden, feats, time, mixed, table, group, dims, after=()):
    rows, width, seqs = dims
    span = rows // seqs
    n = len(group.arrays)
    up, out = 2 * width, width // 2
    wide = up + out

    def kernel(place_ref, bounds_ref, hidden_ref, feats_ref, time_ref, mixed_ref, vec_ref, *refs):
        ins = refs[:n]
        normed_ref, middle_ref, inverse_ref, acted_ref, slope_ref, out_ref, w_ref, branch_ref, sem = refs[n:]
        row = lambda r: vec_ref[r : r + 1, :]
        group.load(ins, place_ref, w_ref, sem)
        for h in range(2):
            out_ref[:, h * out : (h + 1) * out] = columns_of(w_ref, h * wide + up, (h + 1) * wide)
        temb = dot(feats_ref[...], time_ref[...], (1, 1))
        branch_ref[...] = dot(mixed_ref[...], out_ref[...]) + row(BIAS_OUT)

        def use(at, start):
            normed, inverse = norm_parts(start + branch_ref[at, :])
            normed_ref[at, :] = normed
            middle_ref[at, :] = (normed * row(GAIN_MID) + row(SHIFT_MID)).astype(HALF)
            inverse_ref[at, :] = jnp.broadcast_to(inverse, (span, 128))

        add_time(hidden_ref, bounds_ref, temb, seqs, span, use)
        gelu_blocks((0, 1), middle_ref, w_ref, row, acted_ref, slope_ref, width, wide)

    outs = [
        held((rows, width), WIDE),
        held((rows, width)),
        held((rows, 128), WIDE),
        held((rows, 2 * up)),
        held((rows, 2 * up)),
        held((width, width)),
        held(group.dims),
    ]
    return call(
        kernel,
        (1,),
        [SCALARS, SCALARS] + whole_specs([hidden, feats, time, mixed, table]) + [ANYWHERE] * n,
        whole_specs(outs),
        outs,
        [pltpu.VMEM((rows, width), WIDE), pltpu.SemaphoreType.DMA],
        after=after,
        flops=rows * width * width * 6,
        cost=8.7, vmem=10,
    )(place, bounds, hidden, feats, *near(time, mixed, table), *far(*group.arrays))


def gelu_blocks(blocks, middle_ref, w_ref, row, acted_ref, slope_ref, width, wide):
    root = math.sqrt(2 / math.pi)
    for k in blocks:
        low = (k // 2) * wide + (k % 2) * width
        cols = slice(k * width, (k + 1) * width)
        u = dot(middle_ref[...], columns_of(w_ref, low, low + width)) + row(BIAS_UP + k)
        square = u * u
        gate = 0.5 + 0.5 * jnp.tanh(u * (root + (root * 0.044715) * square))
        acted = u * gate
        acted_ref[:, cols] = acted.astype(HALF)
        slope = gate + (acted - acted * gate) * (2 * root + (6 * root * 0.044715) * square)
        slope_ref[:, cols] = slope.astype(HALF)


def raise_rest(middle, table, weight, acted, slope, after=()):
    rows, width = middle.shape
    wide = weight.shape[-1] // 2

    def kernel(middle_ref, vec_ref, w_ref, acted_in, slope_in, acted_ref, slope_ref):
        row = lambda r: vec_ref[r : r + 1, :]
        gelu_blocks((2, 3), middle_ref, w_ref, row, acted_ref, slope_ref, width, wide)

    ins = [middle, table, weight, acted, slope]
    outs = [held(acted.shape), held(slope.shape)]
    return call(
        kernel,
        (1,),
        whole_specs(ins[:3]) + [pl.BlockSpec(memory_space=pltpu.VMEM)] * 2,
        [pl.BlockSpec(memory_space=pltpu.VMEM)] * 2,
        outs,
        after=after,
        aliases={3: 0, 4: 1},
        flops=rows * width * width * 4,
        cost=3.7, vmem=10,
    )(*near(*ins))


def lower(place, lens, acted, slope, normed, cotangent, table, group, dims, away, after=()):
    rows, width, seqs = dims
    span = rows // seqs
    n = len(group.arrays)
    tall = 4 * width

    def kernel(place_ref, lens_ref, away_ref, acted_ref, slope_ref, normed_ref, cot_ref, vec_ref, *refs):
        ins = refs[:n]
        act_ref, back_ref, down_ref, up_ref, sums_ref, sent_ref, w_ref, sem = refs[n:]
        sums_ref[...] = jnp.zeros_like(sums_ref)
        group.load(ins, place_ref, w_ref, sem)
        row = lambda r: vec_ref[r : r + 1, :]

        def count(r, value):
            sums_ref[r : r + 1, :] += jnp.sum(value, 0, keepdims=True)

        back_ref[...] = dot(acted_ref[...], columns_of(w_ref, 0, width)) + row(BIAS_DOWN)
        places = lax.broadcasted_iota(jnp.int32, (span, 1), 0)
        for s in range(seqs):
            at = slice(s * span, (s + 1) * span)
            valid = jnp.where(places < lens_ref[s], 1.0, 0.0)
            middle = normed_ref[at, :] * row(GAIN_MID) + row(SHIFT_MID)
            last, inverse = norm_parts(middle + back_ref[at, :])
            act_ref[at, :] = ((last * row(GAIN_LAST) + row(SHIFT_LAST)) * valid).astype(HALF)
            grad = cot_ref[at, :].astype(WIDE) * valid
            count(GAIN_LAST, grad * last)
            count(SHIFT_LAST, grad)
            back = norm_back(grad * row(GAIN_LAST), last, inverse)
            back_ref[at, :] = back
            down = back.astype(HALF)
            down_ref[at, :] = down
            count(BIAS_DOWN, down.astype(WIDE))
        wide = width // 2
        half = down_ref[:, pl.ds(pl.multiple_of(away_ref[0] * wide, 128), wide)]
        for k in range(4):
            cols = slice(k * width, (k + 1) * width)
            sent_ref[cols, :] = dot(acted_ref[:, cols], half, (0, 0)).astype(HALF)
        weight = columns_of(w_ref, 0, width)
        for k in range(4):
            cols = slice(k * width, (k + 1) * width)
            grad = dot(down_ref[...], weight[cols, :], (1, 1))
            up = (grad * slope_ref[:, cols].astype(WIDE)).astype(HALF)
            up_ref[:, cols] = up
            count(BIAS_UP + k, up.astype(WIDE))

    outs = [
        shape((rows, width)),
        held((rows, width), WIDE),
        held((rows, width)),
        held((rows, tall)),
        held((TALL, width), WIDE),
        shape((tall, width // 2)),
    ]
    return call(
        kernel,
        (1,),
        [SCALARS] * 3 + whole_specs([acted, slope, normed, cotangent, table]) + [ANYWHERE] * n,
        whole_specs(outs),
        outs,
        [pltpu.VMEM(group.dims, HALF), pltpu.SemaphoreType.DMA],
        after=after,
        flops=rows * width * width * 20,
        cost=17.7, vmem=18,
    )(place, lens, away, *near(acted, slope, normed), cotangent, *near(table), *far(*group.arrays))


def back_middle(up_grad, back, normed, inverse, table, sums, weight, dims, after=()):
    rows, width = dims
    up = 2 * width
    wide = up + width // 2
    span = 128

    def kernel(up_ref, back_ref, normed_ref, inverse_ref, vec_ref, before_ref, w_ref, first_ref, branch_ref, sums_ref):
        sums_ref[...] = before_ref[...]
        first_ref[...] = dot(up_ref[:, :up], columns_of(w_ref, 0, up), (1, 1))
        first_ref[...] += dot(up_ref[:, up:], columns_of(w_ref, wide, wide + up), (1, 1))
        gain = vec_ref[GAIN_MID : GAIN_MID + 1, :]
        for s in range(rows // span):
            at = slice(s * span, (s + 1) * span)
            grad = back_ref[at, :] + first_ref[at, :]
            normed = normed_ref[at, :]
            sums_ref[GAIN_MID : GAIN_MID + 1, :] += jnp.sum(grad * normed, 0, keepdims=True)
            sums_ref[SHIFT_MID : SHIFT_MID + 1, :] += jnp.sum(grad, 0, keepdims=True)
            first = norm_back(grad * gain, normed, inverse_ref[at, :1])
            first_ref[at, :] = first
            branch = first.astype(HALF)
            branch_ref[at, :] = branch
            sums_ref[BIAS_OUT : BIAS_OUT + 1, :] += jnp.sum(branch.astype(WIDE), 0, keepdims=True)

    outs = [held((rows, width), WIDE), held((rows, width)), held((TALL, width), WIDE)]
    ins = [up_grad, back, normed, inverse, table, sums, weight]
    return call(
        kernel,
        (1,),
        whole_specs(ins),
        whole_specs(outs),
        outs,
        after=after,
        flops=rows * width * width * 8,
        cost=5.1, vmem=8,
    )(*near(*ins))


def back_attend(lens, branch, qkv, stats, sums, weight, dims, low_seq, high_seq, earlier=None, after=()):
    rows, width, seqs = dims
    span = rows // seqs
    pairs = width // 128
    scale = (width // HEADS) ** (-0.5)
    count = high_seq - low_seq
    top = low_seq * span if earlier is not None else 0
    size = (top + count * span, 3 * width)

    def kernel(lens_ref, branch_ref, qkv_ref, stats_ref, before_ref, w_ref, *refs):
        out_ref, sums_ref, mix_ref = refs[-3:]
        sums_ref[...] = before_ref[...]
        if top:
            out_ref[:top, :] = refs[0][...]
        mix_ref[...] = dot(branch_ref[low_seq * span : high_seq * span, :], w_ref[...], (1, 1)).astype(HALF)
        lane = lax.broadcasted_iota(jnp.int32, (span, 128), 1)
        low = lane < 64

        @pl.loop(0, count)
        def _(s):
            here = pl.ds(pl.multiple_of(s * span, span), span)
            at = pl.ds(pl.multiple_of((s + low_seq) * span, span), span)
            there = pl.ds(pl.multiple_of(s * span + top, span), span)
            keep = lane < lens_ref[s + low_seq]
            for p in range(pairs):
                cols = lambda m: slice(m * width + p * 128, m * width + (p + 1) * 128)
                query, grad = qkv_ref[at, cols(0)], mix_ref[here, cols(0)]
                keys = pair_split(qkv_ref[at, cols(1)], low)
                values = pair_split(qkv_ref[at, cols(2)], low)
                scores = dot(query, keys, (1, 1))
                grad_probs = dot(grad, values, (1, 1))
                probs, dscores = [], []
                for h in range(2):
                    half = slice(h * span, (h + 1) * span)
                    lse = stats_ref[at, 2 * p + h : 2 * p + h + 1]
                    prob = jnp.exp(jnp.where(keep, scores[:, half], -1e30) - lse)
                    product = prob * grad_probs[:, half]
                    delta = jnp.sum(product, -1, keepdims=True)
                    probs.append(prob.astype(HALF))
                    dscores.append((product - prob * delta).astype(HALF))
                probs = jnp.concatenate(probs, axis=1)
                dscores = jnp.concatenate(dscores, axis=1)
                dvalues = dot(probs, grad, (0, 0))
                dkeys = dot(dscores, query, (0, 0))
                dquery = (dot(dscores, keys).astype(HALF).astype(WIDE) * scale).astype(HALF)
                out_ref[there, cols(0)] = dquery
                sums_ref[BIAS_Q : BIAS_Q + 1, cols(0)] += jnp.sum(dquery.astype(WIDE), 0, keepdims=True)
                dkeys = jnp.where(low, dkeys[:span], dkeys[span:]).astype(HALF)
                out_ref[there, cols(1)] = dkeys
                dvalues = jnp.where(low, dvalues[:span], dvalues[span:]).astype(HALF)
                out_ref[there, cols(2)] = dvalues
                sums_ref[BIAS_V : BIAS_V + 1, cols(0)] += jnp.sum(dvalues.astype(WIDE), 0, keepdims=True)

    ins = [branch, qkv, stats, sums, weight] + ([earlier] if top else [])
    outs = [held(size), held((TALL, width), WIDE)]
    return call(
        kernel,
        (1,),
        [SCALARS] + whole_specs(ins),
        whole_specs(outs),
        outs,
        [pltpu.VMEM((count * span, width), HALF)],
        after=after,
        flops=rows * width * width * 4,
        cost=7.5, vmem=6,
    )(lens, *near(*ins))


def back_start(bounds, place, dproj, first, feats, sums, weight, dims, shards, after=()):
    rows, width, seqs = dims
    span = rows // seqs
    half = 3 * width // 2
    wide = half + TFREQ

    def kernel(bounds_ref, place_ref, dproj_ref, first_ref, feats_ref, sums_ref, w_ref, hidden_ref, *refs):
        acc_ref, temb_ref = refs[-2:]
        more_ref = refs[0]
        acc_ref[...] = dot(dproj_ref[:, :half], columns_of(w_ref, 0, half), (1, 1))
        acc_ref[...] += dot(dproj_ref[:, half:], columns_of(w_ref, wide, wide + half), (1, 1))
        temb_ref[...] = jnp.zeros_like(temb_ref)
        places = lax.broadcasted_iota(jnp.int32, (span, 1), 0)
        for s in range(seqs):
            at = slice(s * span, (s + 1) * span)
            grad = acc_ref[at, :] + first_ref[at, :]
            hidden_ref[at, :] = grad.astype(HALF)
            target = jnp.where(places >= bounds_ref[s], 1.0, 0.0)
            temb_ref[s : s + 1, :] = jnp.sum(grad * target, 0, keepdims=True)
        grad = lax.dot_general(
            temb_ref[...],
            feats_ref[...].astype(WIDE),
            (((0,), (0,)), ((), ())),
            precision=lax.Precision.HIGHEST,
            preferred_element_type=WIDE,
        )
        if not shards:
            more_ref[...] = grad
            return
        grad = grad.astype(HALF)
        pieces = pieces_of(sums_ref[...].astype(HALF), width, shards).reshape(shards, TALL, TFREQ)
        rest = jnp.zeros((shards, width // shards - TALL, TFREQ), HALF)
        pieces = jnp.concatenate([pieces, rest], axis=1).reshape(width, TFREQ)
        first_half = place_ref[3] == 0
        more_ref[...] = jnp.where(first_half, grad, pieces)
        refs[1][...] = jnp.where(first_half, pieces, grad)

    outs = [shape((rows, width))]
    outs += [held((width, TFREQ)), shape((width, TFREQ))] if shards else [shape((width, TFREQ), WIDE)]
    ins = [dproj, first, feats, sums, weight]
    return call(
        kernel,
        (1,),
        [SCALARS, SCALARS] + whole_specs(ins),
        whole_specs(outs),
        outs,
        [pltpu.VMEM((rows, width), WIDE), pltpu.VMEM(feats.shape[:1] + (width,), WIDE)],
        after=after,
        flops=rows * width * width * 6,
        cost=5.7, vmem=8,
    )(bounds, place, *near(dproj, first), feats, *near(sums, weight))


def half_of(ref, half):
    wide = ref.shape[1] // 2
    return ref[:, pl.ds(pl.multiple_of(half * wide, 128), wide)]


def outer(half, pairs, after=()):
    columns = [r.shape[1] // 2 for _, r in pairs]
    tall = pairs[0][0].shape[1]

    def kernel(half_ref, *refs):
        out_ref, low = refs[-1], 0
        for n, wide in enumerate(columns):
            right = half_of(refs[2 * n + 1], half_ref[0])
            out_ref[:, low : low + wide] = dot(refs[2 * n][...], right, (0, 0)).astype(HALF)
            low += wide

    ins = sum([[l, r] for l, r in pairs], [])
    return call(
        kernel,
        (1,),
        whole_specs(ins),
        fixed((tall, sum(columns))),
        shape((tall, sum(columns))),
        prefetch=(half,),
        after=after,
        flops=sum(2 * l.shape[0] * tall * c for (l, _), c in zip(pairs, columns)),
        cost=2.8, vmem=8,
    )(*near(*ins))


def keep_outer(half, spot, pairs, arrived, zs, extras=None, after=()):
    columns = [r.shape[1] // 2 for _, r in pairs]
    tall = pairs[0][0].shape[1]
    wide = sum(columns) + (TFREQ if extras else 0)
    each = tall // (zs * XS * 2)
    low_zs = zs // 2
    count = len(pairs)

    def kernel(half_ref, spot_ref, *refs):
        ins, refs = refs[: 2 * count], refs[2 * count :]
        arrived_ref, refs = refs[0], refs[1:]
        if extras:
            (more_ref, more_arrived), refs = refs[:2], refs[2:]
        outs, value_ref, sems = refs[:5], refs[5], refs[6]
        x0, y0 = spot_ref[1], spot_ref[2]

        def put(value, low, high):
            value_ref[..., low:high] = value.astype(HALF).reshape(zs, XS, 2, each, high - low)

        low = 0
        for n, high in enumerate(columns):
            high += low
            right = half_of(ins[2 * n + 1], half_ref[0])
            put(dot(ins[2 * n][...], right, (0, 0)) + arrived_ref[:, low:high].astype(WIDE), low, high)
            low = high
        if extras:
            put(more_ref[...].astype(WIDE) + more_arrived[...].astype(WIDE), low, low + TFREQ)
        own, by_x, by_y, x_later, y_later = outs
        rest = zs - low_zs
        lows, highs = pl.ds(0, low_zs), pl.ds(low_zs, rest)
        x1, y1 = 1 - x0, 1 - y0
        moves = [
            ((pl.ds(0, zs), x0, y0), own),
            ((lows, x1, y1), by_x.at[pl.ds(0, low_zs)]),
            ((lows, x1, y0), by_x.at[pl.ds(low_zs, low_zs)]),
            ((highs, x1, y1), by_y.at[pl.ds(0, rest)]),
            ((highs, x0, y1), by_y.at[pl.ds(rest, rest)]),
            ((highs, x1, y0), x_later),
            ((lows, x0, y1), y_later),
        ]
        load([pltpu.make_async_copy(value_ref.at[cut], o, sems.at[n]) for n, (cut, o) in enumerate(moves)])

    ins = sum([[l, r] for l, r in pairs], [])
    rest = [arrived] + (list(extras) if extras else [])
    sizes = [(k, each, wide) for k in (zs, 2 * low_zs, 2 * (zs - low_zs), zs - low_zs, low_zs)]
    return call(
        kernel,
        (1,),
        whole_specs(ins + rest),
        [ANYWHERE] * len(sizes),
        [shape(s) for s in sizes],
        [pltpu.VMEM((zs, XS, 2, each, wide), HALF), pltpu.SemaphoreType.DMA((7,))],
        prefetch=(half, spot),
        after=after,
        flops=sum(2 * l.shape[0] * tall * c for (l, _), c in zip(pairs, columns)),
        cost=4.3, vmem=14,
    )(*near(*ins), *rest)


def plain_outer(left, right):
    return dot(left, right, (0, 0)).astype(HALF)


class Routes:
    def __init__(self, shards, reps):
        self.shards, self.reps, self.zs = shards, reps, shards // XS

    def core(self, value):
        return lax.ppermute(value, "rep", [(r, r ^ 1) for r in range(self.reps)])

    def y(self, value):
        return lax.ppermute(value, "rep", [(r, r ^ 2) for r in range(self.reps)])

    def x(self, value):
        return lax.ppermute(value, "fsdp", [(f, f ^ 1) for f in range(self.shards)])

    def shift(self, value, step):
        return lax.ppermute(value, "fsdp", [(f, (f + step * XS) % self.shards) for f in range(self.shards)])

    def z(self, value):
        lines = [[z * XS + x for z in range(self.zs)] for x in range(XS)]
        return lax.all_to_all(value, "fsdp", 0, 0, axis_index_groups=lines, tiled=True)


def z(self, value, step):
        return lax.ppermute(
            value, "fsdp", [(f, (f + step * XS) % self.shards) for f in range(self.shards)]
        )


def prepare(spot, qkv, time, small, up, out, down, zs):
    cut, part = qkv.shape[0] // 2, qkv.shape[0]
    tall = down.shape[0] // 2
    third = down.shape[1] // 2
    halves = [v.shape[1] // 2 for v in (qkv, up, out)]
    widths = [halves[0] + TFREQ, halves[1] + halves[2], tall // cut * third]
    n = len(small)

    def kernel(spot_ref, qkv_ref, time_ref, up_ref, out_ref, down_ref, *refs):
        vecs, outs, table_ref, kept, sem = refs[:n], refs[n : n + 3], refs[n + 3], refs[n + 4 : -1], refs[-1]
        load([pltpu.make_async_copy(v, h, sem.at[i]) for i, (v, h) in enumerate(zip(vecs, kept))])
        table_ref[...] = jnp.zeros_like(table_ref)
        top = 0
        for ref in kept:
            value = ref[...].astype(WIDE).reshape(1, ref.shape[0])
            for m in range(ref.shape[0] // part):
                table_ref[top : top + 1, :part] = value[:, m * part : (m + 1) * part]
                top += 1
        table = jnp.where(spot_ref[2] == 0, table_ref[...], 0.0).astype(HALF)
        first = [qkv_ref[...], jnp.where(spot_ref[3] == 0, time_ref[...], table)]
        third_parts = [down_ref[i * cut : (i + 1) * cut, :] for i in range(tall // cut)]
        for ref, parts in zip(outs, (first, [up_ref[...], out_ref[...]], third_parts)):
            here = 0
            for value in parts:
                there = slice(here, here + value.shape[1])
                if len(ref.shape) == 2:
                    ref[:, there] = value
                else:
                    for k in range(zs):
                        ref[k, :, there] = value
                here += value.shape[1]

    quarter = lambda rows, columns: pl.BlockSpec((rows, columns), lambda i, spot: (spot[2], spot[3]))
    sizes = [(zs, cut, w) if at_once else (cut, w) for w, at_once in zip(widths, (False, False, False))]
    return call(
        kernel,
        (1,),
        [
            quarter(cut, halves[0]),
            pl.BlockSpec((cut, TFREQ), lambda i, spot: (spot[2], 0)),
            quarter(cut, halves[1]),
            quarter(cut, halves[2]),
            quarter(tall, third),
        ]
        + [ANYWHERE] * n,
        [fixed(s) for s in sizes],
        [shape(s) for s in sizes],
        [pltpu.VMEM((cut, TFREQ), WIDE)]
        + [pltpu.VMEM(v.shape, HALF) for v in small]
        + [pltpu.SemaphoreType.DMA((n,))],
        prefetch=(spot,),
        cost=3, vmem=6,
    )(*far(qkv, time, up, out, down, *small))


def weave(spot, zs, arrays, outs, after=()):
    arrays = list(arrays)

    def kernel(spot_ref, *refs):
        for ref, (copies, parts) in zip(refs[len(arrays) :], outs):
            here = 0
            for n, low, count, step in parts:
                cols = slice(low, low + count)
                value = refs[n][:, cols] if step is None else refs[n][lax.rem(spot_ref[0] + (zs - step), zs), :, cols]
                there = slice(here, here + count)
                if copies is None:
                    ref[:, there] = value
                else:
                    for k in range(copies):
                        ref[k, :, there] = value
                here += count

    rows = arrays[0].shape[-2]
    sizes = [(() if c is None else (c,)) + (rows, sum(p[2] for p in parts)) for c, parts in outs]
    return call(
        kernel,
        (1,),
        [SCALARS] + whole_specs(arrays),
        [fixed(s) for s in sizes],
        [shape(s) for s in sizes],
        after=after,
        cost=0.8, vmem=8,
    )(spot, *arrays)


def cut_of(layout, low, high, dx, dy):
    out, left = [], 0
    for g, dz, count in layout:
        first, last = max(low, left), min(high, left + count)
        if first < last:
            out.append((g, dz, dx, dy, first - left, last - first))
        left += count
    return out


def middle_of(count):
    return count // 2 // 128 * 128


class Gather:
    def __init__(self, spot, owns, routes):
        self.spot, self.routes = spot, routes
        self.widths = [o.shape[-1] for o in owns]
        self.arrays, self.segments = [], [[] for _ in self.widths]
        shifts = lambda o: [o] + [routes.shift(o, step) for step in range(1, routes.zs)]
        self.by_z = [shifts(o) if o.ndim == 2 else [routes.z(o)] for o in owns]
        self.line = [None] * len(owns)

    def weave(self, arrays, outs, after=()):
        return weave(self.spot, self.routes.zs, arrays, outs, after)

    def add(self, array, parts, dc=0):
        low = 0
        for g, dz, dx, dy, column, count in parts:
            self.segments[g].append((len(self.arrays), low, count, dz, dx, dy, dc, column))
            low += count
        self.arrays.append(array)

    def both(self, array, parts):
        core = self.routes.core(array)
        self.add(array, parts)
        self.add(core, parts, 1)
        return core

    def group(self, g, dims):
        used = sorted({s[0] for s in self.segments[g]})
        segments = [(used.index(s[0]),) + s[1:] for s in self.segments[g]]
        return Gathered([self.arrays[n] for n in used], segments, dims)

    def follow(self, g, after=()):
        come, width = self.by_z[g], self.widths[g]
        if len(come) > 1:
            lines = [(step, 0, width, None) for step in range(self.routes.zs)]
        else:
            lines = [(0, 0, width, step) for step in range(self.routes.zs)]
        (line,) = self.weave(come, [(None, lines)], after)
        self.line[g] = [line, self.routes.x(line), self.routes.y(line)]
        return line

    def onward(self, g, after=()):
        whole = [(g, step, self.widths[g]) for step in range(self.routes.zs)]
        count = self.routes.zs * self.widths[g]
        cut = middle_of(count)
        x2, y2, known = self.weave(
            self.line[g],
            [
                (None, [(2, 0, cut, None)]),
                (None, [(1, cut, count - cut, None)]),
                (None, [(k, 0, count, None) for k in range(3)]),
            ],
            after,
        )
        sent = x2
        x2, y2 = self.routes.x(x2), self.routes.y(y2)
        self.both(known, sum([cut_of(whole, 0, count, dx, dy) for dx, dy in ((0, 0), (1, 0), (0, 1))], []))
        self.both(x2, cut_of(whole, 0, cut, 1, 1))
        self.both(y2, cut_of(whole, cut, count, 1, 1))
        self.passed = [x2, y2]
        return sent


def total(*terms):
    return functools.reduce(lambda a, b: a + b, [t.astype(WIDE) for t in terms]).astype(HALF)


def first_hop(kept, routes):
    own, by_x, by_y, x_later, y_later = kept
    return own, routes.x(by_x), routes.y(by_y), x_later, y_later


def second_hop(state, routes, after=()):
    own, from_x, from_y, x_later, y_later = state
    rest, low = x_later.shape[0], y_later.shape[0]

    def kernel(from_x_ref, from_y_ref, x_ref, y_ref, x_out, y_out):
        x_out[...] = total(x_ref[...], from_y_ref[:rest])
        y_out[...] = total(y_ref[...], from_x_ref[:low])

    ins = (from_x, from_y, x_later, y_later)
    outs = [shape(x_later.shape), shape(y_later.shape)]
    x_later, y_later = call(kernel, (1,), whole_specs(ins), whole_specs(outs), outs, after=after, cost=0.5, vmem=6)(*ins)
    return own, from_x, from_y, routes.x(x_later), routes.y(y_later), x_later


def line_sum(state, after=()):
    state = state[:5]
    own, _, _, x_late, y_late = state
    low, rest = y_late.shape[0], x_late.shape[0]

    def kernel(own_ref, from_x, from_y, x_late, y_late, out_ref):
        out_ref[:low] = total(own_ref[:low], from_x[low:], y_late[...])
        out_ref[low:] = total(own_ref[low:], x_late[...], from_y[rest:])

    return call(
        kernel, (1,), whole_specs(state), fixed(own.shape), shape(own.shape), after=after, cost=0.5, vmem=8
    )(*state)


def last_hops(line, routes, after=()):
    came = routes.z(line)

    def kernel(came_ref, out_ref):
        out_ref[...] = total(*[came_ref[k] for k in range(came.shape[0])])

    size = came.shape[1:]
    mine = call(kernel, (1,), whole_specs([came]), fixed(size), shape(size), after=after, cost=0.5, vmem=4)(came)
    other = routes.y(mine)
    return [mine, routes.core(mine), other, routes.core(other)]


def in_order(pieces, y0, c0):
    rows = [
        [jnp.where(c0 == 0, a, b), jnp.where(c0 == 0, b, a)] for a, b in (pieces[0:2], pieces[2:4])
    ]
    return [
        [jnp.where(y0 == 0, rows[y][c], rows[1 - y][c]) for c in range(2)] for y in range(2)
    ]


def finish(spot, pieces, cuts, outs, vectors=(), after=()):
    rows = pieces[0].shape[0]
    count = len(outs)

    def kernel(spot_ref, *refs):
        ins, dests, small = refs[:4], refs[4 : 4 + count], refs[4 + count :]
        grid = in_order([r[...] for r in ins], spot_ref[2], spot_ref[3])
        for y in range(2):
            for c, low, wide, out, column in cuts:
                dests[out][y * rows : (y + 1) * rows, column : column + wide] = grid[y][c][
                    :, low : low + wide
                ].astype(WIDE)
        top = 0
        if small:
            table = grid[0][1][:TALL, -TFREQ:].astype(WIDE)
        for ref in small:
            each = vectors[0]
            n = ref.shape[0] // each
            parts = [table[r : r + 1, :each] for r in range(top, top + n)]
            ref[...] = jnp.concatenate(parts, axis=1).reshape(n * each)
            top += n

    lengths = list(vectors[1]) if vectors else []
    return call(
        kernel,
        (1,),
        [SCALARS] + [fixed(v.shape) for v in pieces],
        [fixed(o) for o in outs] + [fixed((n,)) for n in lengths],
        [shape(o, WIDE) for o in outs] + [shape((n,), WIDE) for n in lengths],
        after=after,
        cost=1.7, vmem=12,
    )(spot, *pieces)


def pair_split(value, low):
    zero = jnp.zeros_like(value)
    return jnp.concatenate([jnp.where(low, value, zero), jnp.where(low, zero, value)], axis=0)


def time_features(timesteps):
    half = TFREQ // 2
    freqs = jnp.exp(-math.log(10000.0) * jnp.arange(half).astype(WIDE) / half)
    angles = timesteps.astype(WIDE)[:, None] * freqs[None, :]
    return jnp.concatenate([jnp.cos(angles), jnp.sin(angles)], axis=1)


def layer(
    hidden,
    cotangent,
    lengths,
    bounds,
    timesteps,
    weight_qkv,
    bias_qv,
    weight_out,
    bias_out,
    gain_mid,
    shift_mid,
    weight_up,
    bias_up,
    weight_down,
    bias_down,
    gain_last,
    shift_last,
    weight_time,
):
    shards, reps = lax.axis_size("fsdp"), lax.axis_size("rep")
    rows, width = hidden.shape
    seqs = lengths.shape[0]
    part = weight_out.shape[0]
    by_hand = reps == 4 and shards == 8 and part == 96
    rep, shard = lax.axis_index("rep"), lax.axis_index("fsdp")
    spot = jnp.stack([shard // XS, shard % XS, rep // 2, rep % 2]).astype(jnp.int32)
    small = [bias_qv, bias_out, gain_mid, shift_mid, bias_up, bias_down, gain_last, shift_last]
    feats = jnp.pad(time_features(timesteps).astype(HALF), ((0, -seqs % 8), (0, 0)))
    half, out = 3 * width // 2, width // 2
    known = None
    if by_hand:
        routes = Routes(shards, reps)
        zs = routes.zs
        owns = prepare(spot, weight_qkv, weight_time, small, weight_up, weight_out, weight_down, zs)
        gather = Gather(spot, owns, routes)
        places, cut = (zs, XS, 2), part // 2
        gather.follow(0)
        gather.onward(0, gather.by_z[1])
        sent = gather.follow(1, gather.passed)
        group1 = gather.group(0, places + (cut, 2 * gather.widths[0]))
    else:
        whole = lambda v: lax.all_gather(v, "fsdp", axis=0, tiled=True)
        qkv, up, output = whole(weight_qkv), whole(weight_up), whole(weight_out)
        blank = jnp.zeros((width, TFREQ), HALF)
        group1 = Whole(jnp.concatenate([qkv[:, :half], blank, qkv[:, half:], blank], axis=1))
        group2 = Whole(
            jnp.concatenate([up[:, : 2 * width], output[:, :out], up[:, 2 * width :], output[:, out:]], axis=1)
        )
        group3 = Whole(whole(weight_down))
        table = jnp.concatenate([whole(v).reshape(-1, width) for v in small]).astype(WIDE)
        known = (whole(weight_time), jnp.pad(table, ((0, TALL - table.shape[0]), (0, 0))))

    per_seq, flat = (rows, width, seqs), (rows, width)
    start_b, qkv, table, time, whole1 = project(
        spot, bounds, hidden, feats, group1, known, per_seq, after=[sent] if by_hand else ()
    )
    mixed, stats = attend(lengths, qkv, per_seq)
    if by_hand:
        sent = gather.follow(2, [gather.onward(1, [mixed] + gather.by_z[2])])
        group2 = gather.group(1, places + (cut, 2 * gather.widths[1]))
    normed, middle, inverse, acted, slope, whole_out, whole2 = raise_up(
        spot, bounds, hidden, feats, time, mixed, table, group2, per_seq, after=[sent] if by_hand else ()
    )
    if by_hand:
        sent = gather.onward(2, [middle])
        group3 = gather.group(2, places + (weight_down.shape[0] // 2, width))
    acted, slope = raise_rest(middle, table, whole2, acted, slope, after=[sent] if by_hand else ())
    mine, away = spot[3:], 1 - spot[3:]
    activations, back, down, up_grad, sums, sent = lower(
        spot, lengths, acted, slope, normed, cotangent, table, group3, per_seq, away
    )
    first, branch, sums = back_middle(up_grad, back, normed, inverse, table, sums, whole2, flat)
    if by_hand:
        kept3 = keep_outer(mine, spot, [(acted, down)], routes.core(sent), zs, after=[branch])
        pairs2 = [(middle, up_grad), (mixed, branch)]
        sent = outer(away, pairs2, after=[kept3[0]])
        early, sums = back_attend(
            lengths, branch, qkv, stats, sums, whole_out, per_seq, 0, seqs // 2, after=[sent]
        )
        kept2 = keep_outer(mine, spot, pairs2, routes.core(sent), zs, after=[early])
        state3 = second_hop(first_hop(kept3, routes), routes, after=[kept2[0]])
        dproj, sums = back_attend(
            lengths, branch, qkv, stats, sums, whole_out, per_seq, seqs // 2, seqs, early, after=[state3[-1]]
        )
        terms3 = line_sum(state3, after=[dproj])
        sent = outer(away, [(start_b, dproj)], after=[terms3])
        state2 = second_hop(first_hop(kept2, routes), routes, after=[sent])
    else:
        dproj, sums = back_attend(lengths, branch, qkv, stats, sums, whole_out, per_seq, 0, seqs)
    grad_hidden, extras, *more = back_start(
        bounds, spot, dproj, first, feats, sums, whole1, per_seq, shards if by_hand else 0, after=[state2[-1]] if by_hand else ()
    )
    if by_hand:
        extra_sent = routes.core(more[0])
        sums3 = last_hops(terms3, routes, after=[grad_hidden])
        terms2 = line_sum(state2, after=[sums3[0]])
        kept1 = keep_outer(
            mine, spot, [(start_b, dproj)], routes.core(sent), zs, (extras, extra_sent), after=[terms2]
        )
        (out_down,) = finish(
            spot, sums3, [(c, 0, out, 0, c * out) for c in range(2)], [weight_down.shape], after=[kept1[0]]
        )
        sums2 = last_hops(terms2, routes, after=[out_down])
        state1 = second_hop(first_hop(kept1, routes), routes, after=[sums2[0]])
        out_up, out_out = finish(
            spot,
            sums2,
            [(c, 0, 2 * width, 0, c * 2 * width) for c in range(2)]
            + [(c, 2 * width, out, 1, c * out) for c in range(2)],
            [weight_up.shape, weight_out.shape],
            after=[state1[-1]],
        )
        terms1 = line_sum(state1, after=[out_up])
        out_qkv, out_time, *out_small = finish(
            spot,
            last_hops(terms1, routes),
            [(c, 0, half, 0, c * half) for c in range(2)] + [(0, half, TFREQ, 1, 0)],
            [weight_qkv.shape, weight_time.shape],
            (part, [v.shape[0] for v in small]),
        )
    else:

        def summed(v):
            v = lax.psum_scatter(v.astype(HALF), "fsdp", scatter_dimension=0, tiled=True)
            return lax.psum(v, "rep").astype(WIDE)

        out_qkv, out_out = summed(plain_outer(start_b, dproj)), summed(plain_outer(mixed, branch))
        out_up, out_down = summed(plain_outer(middle, up_grad)), summed(plain_outer(acted, down))
        out_time = summed(extras)
        counts = [v.shape[0] * shards // width for v in small]
        tops = [sum(counts[:i]) for i in range(len(counts))]
        out_small = [summed(sums[t : t + n].reshape(-1)) for t, n in zip(tops, counts)]
    return (
        activations,
        grad_hidden,
        out_qkv,
        out_small[0],
        out_out,
        out_small[1],
        out_small[2],
        out_small[3],
        out_up,
        out_small[4],
        out_down,
        out_small[5],
        out_small[6],
        out_small[7],
        out_time,
    )


def solution(mesh):
    tokens, table, vector = P(("rep", "fsdp"), None), P("fsdp", None), P("fsdp")
    per_sequence = P(("rep", "fsdp"))
    weights = (table, vector, table, vector, vector, vector, table, vector, table, vector, vector, vector, table)
    return jax.shard_map(
        layer,
        mesh=mesh,
        in_specs=(tokens, tokens, per_sequence, per_sequence, per_sequence) + weights,
        out_specs=(tokens, tokens) + weights,
        check_vma=False,
    )
```

```python
import functools
import math

import jax
import jax.numpy as jnp
from jax import lax
from jax.experimental import pallas as pl
from jax.experimental.pallas import tpu as pltpu
from jax.sharding import PartitionSpec as P

HEADS = 12
TFREQ = 128
XS = 2
TALL = 16
WIDE = jnp.float32
HALF = jnp.bfloat16
MIB = 1024 * 1024
(BIAS_Q, BIAS_V, BIAS_OUT, GAIN_MID, SHIFT_MID, BIAS_UP, BIAS_DOWN, GAIN_LAST, SHIFT_LAST) = (0, 1, 2, 3, 4, 5, 9, 10, 11)

ANYWHERE = pl.BlockSpec(memory_space=pltpu.HBM)
SCALARS = pl.BlockSpec(memory_space=pltpu.SMEM)


def dot(left, right, axes=(1, 0)):
    return lax.dot_general(
        left, right, (((axes[0],), (axes[1],)), ((), ())), preferred_element_type=WIDE
    )


def shape(dims, dtype=HALF):
    return jax.ShapeDtypeStruct(tuple(dims), dtype)


def held(dims, dtype=HALF):
    return pltpu.VMEM(tuple(dims), dtype)


def near(*values):
    return [pltpu.with_memory_space_constraint(v, pltpu.VMEM) for v in values]


def far(*values):
    return [pltpu.with_memory_space_constraint(v, pltpu.HBM) for v in values]


def fixed(dims):
    return pl.BlockSpec(tuple(dims), lambda *_: (0,) * len(dims))


def call(
    kernel, grid, in_specs, out_specs, out_shape, scratch=(), prefetch=(), after=(), aliases=None, vmem=24, cost=1.0, token=False
):
    after = list(after)
    count, n = len(in_specs), len(after)
    if token:
        results = len(out_specs)
        out_specs = list(out_specs) + [fixed((8, 128))]
        out_shape = list(out_shape) + [shape((8, 128), WIDE)]

    def run(*refs):
        start = len(prefetch) + count
        refs = refs[:start] + refs[start + n :]
        if token:
            there = refs[start + results]
            there[...] = jnp.zeros_like(there)
            refs = refs[: start + results] + refs[start + results + 1 :]
        kernel(*refs)

    return lambda *operands: pl.pallas_call(
        run,
        grid_spec=pltpu.PrefetchScalarGridSpec(
            num_scalar_prefetch=len(prefetch),
            grid=grid,
            in_specs=in_specs + [ANYWHERE] * n,
            out_specs=out_specs,
            scratch_shapes=list(scratch),
        ),
        out_shape=out_shape,
        input_output_aliases=aliases or {},
        compiler_params=pltpu.CompilerParams(vmem_limit_bytes=vmem * MIB),
        cost_estimate=pl.CostEstimate(flops=int(cost * 4.0e9), bytes_accessed=int(cost * 4.0e6), transcendentals=0),
    )(*prefetch, *operands, *after)


def norm_parts(value):
    mean = jnp.mean(value, -1, keepdims=True)
    centered = value - mean
    inverse = lax.rsqrt(jnp.mean(centered * centered, -1, keepdims=True) + 1e-05)
    return centered * inverse, inverse


def norm_back(grad, normed, inverse):
    return inverse * (
        grad
        - jnp.mean(grad, -1, keepdims=True)
        - normed * jnp.mean(grad * normed, -1, keepdims=True)
    )


def flip(index, by):
    return 1 - index if by else index


class Gathered:
    def __init__(self, arrays, segments, dims):
        self.arrays, self.segments, self.dims = list(arrays), list(segments), tuple(dims)
        self.zs = dims[0]

    def load(self, refs, place, target, sem):
        zs, _, _, rows, columns = self.dims
        z0, x0, y0, c0 = (place[i] for i in range(4))
        wide = columns // 2
        cut = self.arrays[0].shape[0]
        for n, low, count, dz, dx, dy, dc, column in self.segments:
            z = lax.rem(z0 + (zs - dz), zs)
            while count:
                block = column // wide
                step = min(count, (block + 1) * wide - column)
                first = pl.multiple_of(flip(c0, dc) * wide + column % wide, 128)
                there = target.at[
                    z, flip(x0, dx), flip(y0, dy), pl.ds(block * cut, cut), pl.ds(first, step)
                ]
                pltpu.make_async_copy(refs[n].at[:, pl.ds(low, step)], there, sem).start()
                low, column, count = low + step, column + step, count - step
        pltpu.make_async_copy(target, target, sem).wait()


class Whole:
    def __init__(self, array):
        self.arrays, self.dims = [array], array.shape

    def load(self, refs, place, target, sem):
        copy = pltpu.make_async_copy(refs[0], target, sem)
        copy.start()
        copy.wait()


def load(copies):
    for copy in copies:
        copy.start()
    for copy in copies:
        copy.wait()


def columns_of(ref, low, high):
    value = ref[..., low:high]
    return value.reshape(-1, high - low)


def whole_specs(values):
    return [fixed(v.shape) for v in values]


def vector_map(shards):
    index = lax.broadcasted_iota(jnp.int32, (TALL * shards, 1), 0)
    shard, r = index // TALL, index % TALL
    half, quarter = shards // 2, shards // 4
    query, up = r < 2, (r >= BIAS_UP) & (r < BIAS_DOWN)
    kinds = jnp.where(query, shard // half, jnp.where(up, BIAS_UP + shard // quarter, r))
    spots = jnp.where(
        query, 2 * (shard % half) + r, jnp.where(up, 4 * (shard % quarter) + r - BIAS_UP, shard)
    )
    return kinds, spots


def selector(width, shards):
    each = width // shards
    row = lax.broadcasted_iota(jnp.int32, (width, shards * TFREQ), 0)
    column = lax.broadcasted_iota(jnp.int32, (width, shards * TFREQ), 1)
    lane = column % TFREQ
    return ((row == (column // TFREQ) * each + lane) & (lane < each)).astype(HALF)


def kind_rows(kinds, shards):
    return (kinds == lax.broadcasted_iota(jnp.int32, (TALL * shards, TALL), 1)).astype(HALF)


def table_of(pieces, width, shards):
    kinds, spots = vector_map(shards)
    wide = jnp.concatenate([jnp.where(spots == m, pieces, jnp.zeros_like(pieces)) for m in range(shards)], axis=1)
    spread = dot(wide, selector(width, shards), (1, 1)).astype(HALF)
    return dot(kind_rows(kinds, shards), spread, (0, 0))


def pieces_of(table, width, shards):
    kinds, spots = vector_map(shards)
    spread = dot(dot(kind_rows(kinds, shards), table).astype(HALF), selector(width, shards))
    out = jnp.zeros((TALL * shards, TFREQ), WIDE)
    for m in range(shards):
        out = jnp.where(spots == m, spread[:, m * TFREQ : (m + 1) * TFREQ], out)
    return out.astype(HALF)


def add_time(start_of, bounds_ref, temb, seqs, span, use):
    places = lax.broadcasted_iota(jnp.int32, (span, 1), 0)
    for s in range(seqs):
        at = slice(s * span, (s + 1) * span)
        target = jnp.where(places >= bounds_ref[s], 1.0, 0.0)
        use(at, start_of[at, :].astype(WIDE) + target * temb[s : s + 1, :])


def project(place, bounds, hidden, feats, group, known, dims, after=()):
    rows, width, seqs = dims
    span = rows // seqs
    half = 3 * width // 2
    scale = (width // HEADS) ** (-0.5)
    n = len(group.arrays)
    wide = half + TFREQ

    def kernel(place_ref, bounds_ref, hidden_ref, feats_ref, *refs):
        ins, refs = refs[:n], refs[n:]
        if known:
            time_in, vec_in = refs[:2]
            refs = refs[2:]
        start_ref, qkv_ref, vec_ref, time_ref, w_ref, sem = refs
        group.load(ins, place_ref, w_ref, sem)
        if known:
            time_ref[...], table = time_in[...], vec_in[...]
        else:
            time_ref[...] = columns_of(w_ref, half, wide)
            shards = group.zs * XS
            pieces = columns_of(w_ref, wide + half, 2 * wide).reshape(shards, width // shards, TFREQ)
            table = table_of(pieces[:, :TALL].reshape(shards * TALL, TFREQ), width, shards)
        vec_ref[...] = table
        temb = dot(feats_ref[...], time_ref[...], (1, 1))

        def use(at, start):
            start_ref[at, :] = start.astype(HALF)

        add_time(hidden_ref, bounds_ref, temb, seqs, span, use)
        start_b = start_ref[...]
        first = dot(start_b, columns_of(w_ref, 0, half))
        qkv_ref[:, :width] = ((first[:, :width] + table[BIAS_Q : BIAS_Q + 1]) * scale).astype(HALF)
        qkv_ref[:, width:half] = first[:, width:].astype(HALF)
        second = dot(start_b, columns_of(w_ref, wide, wide + half))
        rest = half - width
        qkv_ref[:, half : half + rest] = second[:, :rest].astype(HALF)
        qkv_ref[:, 2 * width :] = (second[:, rest:] + table[BIAS_V : BIAS_V + 1]).astype(HALF)

    extra = list(known) if known else []
    outs = [held((rows, width)), held((rows, 3 * width)), held((TALL, width), WIDE), held((width, TFREQ)), held(group.dims)]
    return call(
        kernel,
        (1,),
        [SCALARS, SCALARS] + whole_specs([hidden, feats]) + [ANYWHERE] * n + whole_specs(extra),
        whole_specs(outs),
        outs,
        [pltpu.SemaphoreType.DMA],
        after=after,
        cost=0.4375, vmem=6,
    )(place, bounds, hidden, feats, *far(*group.arrays), *extra)


def attend(lens, qkv, dims, after=()):
    rows, width, seqs = dims
    span = rows // seqs
    pairs = width // 128

    def kernel(lens_ref, qkv_ref, mixed_ref, stats_ref):
        lane = lax.broadcasted_iota(jnp.int32, (span, 128), 1)
        low = lane < 64

        @pl.loop(0, seqs)
        def _(s):
            at = pl.ds(pl.multiple_of(s * span, span), span)
            keep = lane < lens_ref[s]
            stats = jnp.zeros((span, 128), WIDE)
            for p in range(pairs):
                cols = lambda m: slice(m * width + p * 128, m * width + (p + 1) * 128)
                keys = pair_split(qkv_ref[at, cols(1)], low)
                values = pair_split(qkv_ref[at, cols(2)], low)
                scores = dot(qkv_ref[at, cols(0)], keys, (1, 1))
                probs = []
                for h in range(2):
                    one = jnp.where(keep, scores[:, h * span : (h + 1) * span], -1e30)
                    top = jnp.max(one, -1, keepdims=True)
                    expo = jnp.exp(one - top)
                    total = jnp.sum(expo, -1, keepdims=True)
                    probs.append((expo * (1.0 / total)).astype(HALF))
                    stats = jnp.where(lane == 2 * p + h, top + jnp.log(total), stats)
                mixed_ref[at, cols(0)] = dot(jnp.concatenate(probs, axis=1), values).astype(HALF)
            stats_ref[at, :] = stats

    outs = [held((rows, width)), held((rows, 128), WIDE)]
    return call(
        kernel,
        (1,),
        [SCALARS] + whole_specs([qkv]),
        whole_specs(outs),
        outs,
        after=after,
        cost=0.4375, vmem=4,
    )(lens, *near(qkv))


def raise_up(place, bounds, hidden, feats, time, mixed, table, group, dims, after=()):
    rows, width, seqs = dims
    span = rows // seqs
    n = len(group.arrays)
    up, out = 2 * width, width // 2
    wide = up + out

    def kernel(place_ref, bounds_ref, hidden_ref, feats_ref, time_ref, mixed_ref, vec_ref, *refs):
        ins = refs[:n]
        normed_ref, middle_ref, inverse_ref, acted_ref, slope_ref, out_ref, w_ref, branch_ref, sem = refs[n:]
        row = lambda r: vec_ref[r : r + 1, :]
        group.load(ins, place_ref, w_ref, sem)
        for h in range(2):
            out_ref[:, h * out : (h + 1) * out] = columns_of(w_ref, h * wide + up, (h + 1) * wide)
        temb = dot(feats_ref[...], time_ref[...], (1, 1))
        branch_ref[...] = dot(mixed_ref[...], out_ref[...]) + row(BIAS_OUT)

        def use(at, start):
            normed, inverse = norm_parts(start + branch_ref[at, :])
            normed_ref[at, :] = normed
            middle_ref[at, :] = (normed * row(GAIN_MID) + row(SHIFT_MID)).astype(HALF)
            inverse_ref[at, :] = jnp.broadcast_to(inverse, (span, 128))

        add_time(hidden_ref, bounds_ref, temb, seqs, span, use)
        gelu_blocks((0, 1), middle_ref, w_ref, row, acted_ref, slope_ref, width, wide)

    outs = [
        held((rows, width), WIDE),
        held((rows, width)),
        held((rows, 128), WIDE),
        held((rows, 2 * up)),
        held((rows, 2 * up)),
        held((width, width)),
        held(group.dims),
    ]
    return call(
        kernel,
        (1,),
        [SCALARS, SCALARS] + whole_specs([hidden, feats, time, mixed, table]) + [ANYWHERE] * n,
        whole_specs(outs),
        outs,
        [pltpu.VMEM((rows, width), WIDE), pltpu.SemaphoreType.DMA],
        after=after,
        cost=0.54375, vmem=10,
    )(place, bounds, hidden, feats, *near(time, mixed, table), *far(*group.arrays))


def gelu_blocks(blocks, middle_ref, w_ref, row, acted_ref, slope_ref, width, wide):
    root = math.sqrt(2 / math.pi)
    for k in blocks:
        low = (k // 2) * wide + (k % 2) * width
        cols = slice(k * width, (k + 1) * width)
        u = dot(middle_ref[...], columns_of(w_ref, low, low + width)) + row(BIAS_UP + k)
        square = u * u
        gate = 0.5 + 0.5 * jnp.tanh(u * (root + (root * 0.044715) * square))
        acted = u * gate
        acted_ref[:, cols] = acted.astype(HALF)
        slope = gate + (acted - acted * gate) * (2 * root + (6 * root * 0.044715) * square)
        slope_ref[:, cols] = slope.astype(HALF)


def raise_rest(middle, table, weight, acted, slope, after=()):
    rows, width = middle.shape
    wide = weight.shape[-1] // 2

    def kernel(middle_ref, vec_ref, w_ref, acted_in, slope_in, acted_ref, slope_ref):
        row = lambda r: vec_ref[r : r + 1, :]
        gelu_blocks((2, 3), middle_ref, w_ref, row, acted_ref, slope_ref, width, wide)

    ins = [middle, table, weight, acted, slope]
    outs = [held(acted.shape), held(slope.shape)]
    return call(
        kernel,
        (1,),
        whole_specs(ins[:3]) + [pl.BlockSpec(memory_space=pltpu.VMEM)] * 2,
        [pl.BlockSpec(memory_space=pltpu.VMEM)] * 2,
        outs,
        after=after,
        aliases={3: 0, 4: 1},
        cost=0.23125, vmem=10,
    )(*near(*ins))


def lower(place, lens, acted, slope, normed, cotangent, table, group, dims, away, after=()):
    rows, width, seqs = dims
    span = rows // seqs
    n = len(group.arrays)
    tall = 4 * width

    def kernel(place_ref, lens_ref, away_ref, acted_ref, slope_ref, normed_ref, cot_ref, vec_ref, *refs):
        ins = refs[:n]
        act_ref, back_ref, down_ref, up_ref, sums_ref, sent_ref, w_ref, sem = refs[n:]
        sums_ref[...] = jnp.zeros_like(sums_ref)
        group.load(ins, place_ref, w_ref, sem)
        row = lambda r: vec_ref[r : r + 1, :]

        def count(r, value):
            sums_ref[r : r + 1, :] += jnp.sum(value, 0, keepdims=True)

        back_ref[...] = dot(acted_ref[...], columns_of(w_ref, 0, width)) + row(BIAS_DOWN)
        places = lax.broadcasted_iota(jnp.int32, (span, 1), 0)
        for s in range(seqs):
            at = slice(s * span, (s + 1) * span)
            valid = jnp.where(places < lens_ref[s], 1.0, 0.0)
            middle = normed_ref[at, :] * row(GAIN_MID) + row(SHIFT_MID)
            last, inverse = norm_parts(middle + back_ref[at, :])
            act_ref[at, :] = ((last * row(GAIN_LAST) + row(SHIFT_LAST)) * valid).astype(HALF)
            grad = cot_ref[at, :].astype(WIDE) * valid
            count(GAIN_LAST, grad * last)
            count(SHIFT_LAST, grad)
            back = norm_back(grad * row(GAIN_LAST), last, inverse)
            back_ref[at, :] = back
            down = back.astype(HALF)
            down_ref[at, :] = down
            count(BIAS_DOWN, down.astype(WIDE))
        wide = width // 2
        half = down_ref[:, pl.ds(pl.multiple_of(away_ref[0] * wide, 128), wide)]
        for k in range(4):
            cols = slice(k * width, (k + 1) * width)
            sent_ref[cols, :] = dot(acted_ref[:, cols], half, (0, 0)).astype(HALF)
        weight = columns_of(w_ref, 0, width)
        for k in range(4):
            cols = slice(k * width, (k + 1) * width)
            grad = dot(down_ref[...], weight[cols, :], (1, 1))
            up = (grad * slope_ref[:, cols].astype(WIDE)).astype(HALF)
            up_ref[:, cols] = up
            count(BIAS_UP + k, up.astype(WIDE))

    outs = [
        shape((rows, width)),
        held((rows, width), WIDE),
        held((rows, width)),
        held((rows, tall)),
        held((TALL, width), WIDE),
        shape((tall, width // 2)),
    ]
    return call(
        kernel,
        (1,),
        [SCALARS] * 3 + whole_specs([acted, slope, normed, cotangent, table]) + [ANYWHERE] * n,
        whole_specs(outs),
        outs,
        [pltpu.VMEM(group.dims, HALF), pltpu.SemaphoreType.DMA],
        after=after,
        cost=17.7, vmem=18,
    )(place, lens, away, *near(acted, slope, normed), cotangent, *near(table), *far(*group.arrays))


def back_middle(up_grad, back, normed, inverse, table, sums, weight, dims, after=()):
    rows, width = dims
    up = 2 * width
    wide = up + width // 2
    span = 128

    def kernel(up_ref, back_ref, normed_ref, inverse_ref, vec_ref, before_ref, w_ref, first_ref, branch_ref, sums_ref):
        sums_ref[...] = before_ref[...]
        first_ref[...] = dot(up_ref[:, :up], columns_of(w_ref, 0, up), (1, 1))
        first_ref[...] += dot(up_ref[:, up:], columns_of(w_ref, wide, wide + up), (1, 1))
        gain = vec_ref[GAIN_MID : GAIN_MID + 1, :]
        for s in range(rows // span):
            at = slice(s * span, (s + 1) * span)
            grad = back_ref[at, :] + first_ref[at, :]
            normed = normed_ref[at, :]
            sums_ref[GAIN_MID : GAIN_MID + 1, :] += jnp.sum(grad * normed, 0, keepdims=True)
            sums_ref[SHIFT_MID : SHIFT_MID + 1, :] += jnp.sum(grad, 0, keepdims=True)
            first = norm_back(grad * gain, normed, inverse_ref[at, :1])
            first_ref[at, :] = first
            branch = first.astype(HALF)
            branch_ref[at, :] = branch
            sums_ref[BIAS_OUT : BIAS_OUT + 1, :] += jnp.sum(branch.astype(WIDE), 0, keepdims=True)

    outs = [held((rows, width), WIDE), held((rows, width)), held((TALL, width), WIDE)]
    ins = [up_grad, back, normed, inverse, table, sums, weight]
    return call(
        kernel,
        (1,),
        whole_specs(ins),
        whole_specs(outs),
        outs,
        after=after,
        cost=5.1, vmem=8,
    )(*near(*ins))


def back_attend(lens, branch, qkv, stats, sums, weight, dims, low_seq, high_seq, earlier=None, after=()):
    rows, width, seqs = dims
    span = rows // seqs
    pairs = width // 128
    scale = (width // HEADS) ** (-0.5)
    count = high_seq - low_seq
    top = low_seq * span if earlier is not None else 0
    size = (top + count * span, 3 * width)

    def kernel(lens_ref, branch_ref, qkv_ref, stats_ref, before_ref, w_ref, *refs):
        out_ref, sums_ref, mix_ref = refs[-3:]
        sums_ref[...] = before_ref[...]
        if top:
            out_ref[:top, :] = refs[0][...]
        mix_ref[...] = dot(branch_ref[low_seq * span : high_seq * span, :], w_ref[...], (1, 1)).astype(HALF)
        lane = lax.broadcasted_iota(jnp.int32, (span, 128), 1)
        low = lane < 64

        @pl.loop(0, count)
        def _(s):
            here = pl.ds(pl.multiple_of(s * span, span), span)
            at = pl.ds(pl.multiple_of((s + low_seq) * span, span), span)
            there = pl.ds(pl.multiple_of(s * span + top, span), span)
            keep = lane < lens_ref[s + low_seq]
            for p in range(pairs):
                cols = lambda m: slice(m * width + p * 128, m * width + (p + 1) * 128)
                query, grad = qkv_ref[at, cols(0)], mix_ref[here, cols(0)]
                keys = pair_split(qkv_ref[at, cols(1)], low)
                values = pair_split(qkv_ref[at, cols(2)], low)
                scores = dot(query, keys, (1, 1))
                grad_probs = dot(grad, values, (1, 1))
                probs, dscores = [], []
                for h in range(2):
                    half = slice(h * span, (h + 1) * span)
                    lse = stats_ref[at, 2 * p + h : 2 * p + h + 1]
                    prob = jnp.exp(jnp.where(keep, scores[:, half], -1e30) - lse)
                    product = prob * grad_probs[:, half]
                    delta = jnp.sum(product, -1, keepdims=True)
                    probs.append(prob.astype(HALF))
                    dscores.append((product - prob * delta).astype(HALF))
                probs = jnp.concatenate(probs, axis=1)
                dscores = jnp.concatenate(dscores, axis=1)
                dvalues = dot(probs, grad, (0, 0))
                dkeys = dot(dscores, query, (0, 0))
                dquery = (dot(dscores, keys).astype(HALF).astype(WIDE) * scale).astype(HALF)
                out_ref[there, cols(0)] = dquery
                sums_ref[BIAS_Q : BIAS_Q + 1, cols(0)] += jnp.sum(dquery.astype(WIDE), 0, keepdims=True)
                dkeys = jnp.where(low, dkeys[:span], dkeys[span:]).astype(HALF)
                out_ref[there, cols(1)] = dkeys
                dvalues = jnp.where(low, dvalues[:span], dvalues[span:]).astype(HALF)
                out_ref[there, cols(2)] = dvalues
                sums_ref[BIAS_V : BIAS_V + 1, cols(0)] += jnp.sum(dvalues.astype(WIDE), 0, keepdims=True)

    ins = [branch, qkv, stats, sums, weight] + ([earlier] if top else [])
    outs = [held(size), held((TALL, width), WIDE)]
    return call(
        kernel,
        (1,),
        [SCALARS] + whole_specs(ins),
        whole_specs(outs),
        outs,
        [pltpu.VMEM((count * span, width), HALF)],
        after=after,
        cost=7.5, vmem=6,
    )(lens, *near(*ins))


def back_start(bounds, place, dproj, first, feats, sums, weight, dims, shards, after=()):
    rows, width, seqs = dims
    span = rows // seqs
    half = 3 * width // 2
    wide = half + TFREQ

    def kernel(bounds_ref, place_ref, dproj_ref, first_ref, feats_ref, sums_ref, w_ref, hidden_ref, *refs):
        acc_ref, temb_ref = refs[-2:]
        more_ref = refs[0]
        acc_ref[...] = dot(dproj_ref[:, :half], columns_of(w_ref, 0, half), (1, 1))
        acc_ref[...] += dot(dproj_ref[:, half:], columns_of(w_ref, wide, wide + half), (1, 1))
        temb_ref[...] = jnp.zeros_like(temb_ref)
        places = lax.broadcasted_iota(jnp.int32, (span, 1), 0)
        for s in range(seqs):
            at = slice(s * span, (s + 1) * span)
            grad = acc_ref[at, :] + first_ref[at, :]
            hidden_ref[at, :] = grad.astype(HALF)
            target = jnp.where(places >= bounds_ref[s], 1.0, 0.0)
            temb_ref[s : s + 1, :] = jnp.sum(grad * target, 0, keepdims=True)
        grad = lax.dot_general(
            temb_ref[...],
            feats_ref[...].astype(WIDE),
            (((0,), (0,)), ((), ())),
            precision=lax.Precision.HIGHEST,
            preferred_element_type=WIDE,
        )
        if not shards:
            more_ref[...] = grad
            return
        grad = grad.astype(HALF)
        pieces = pieces_of(sums_ref[...].astype(HALF), width, shards).reshape(shards, TALL, TFREQ)
        rest = jnp.zeros((shards, width // shards - TALL, TFREQ), HALF)
        pieces = jnp.concatenate([pieces, rest], axis=1).reshape(width, TFREQ)
        first_half = place_ref[3] == 0
        more_ref[...] = jnp.where(first_half, grad, pieces)
        refs[1][...] = jnp.where(first_half, pieces, grad)

    outs = [shape((rows, width))]
    outs += [held((width, TFREQ)), shape((width, TFREQ))] if shards else [shape((width, TFREQ), WIDE)]
    ins = [dproj, first, feats, sums, weight]
    return call(
        kernel,
        (1,),
        [SCALARS, SCALARS] + whole_specs(ins),
        whole_specs(outs),
        outs,
        [pltpu.VMEM((rows, width), WIDE), pltpu.VMEM(feats.shape[:1] + (width,), WIDE)],
        after=after,
        token=True,
        cost=5.7, vmem=8,
    )(bounds, place, *near(dproj, first), feats, *near(sums, weight))


def half_of(ref, half):
    wide = ref.shape[1] // 2
    return ref[:, pl.ds(pl.multiple_of(half * wide, 128), wide)]


def outer(half, pairs, extras=None, after=()):
    columns = [r.shape[1] // 2 for _, r in pairs]
    tall = pairs[0][0].shape[1]
    wide_all = sum(columns) + (TFREQ if extras is not None else 0)

    def kernel(half_ref, *refs):
        out_ref, low = refs[-1], 0
        for n, wide in enumerate(columns):
            right = half_of(refs[2 * n + 1], half_ref[0])
            out_ref[:, low : low + wide] = dot(refs[2 * n][...], right, (0, 0)).astype(HALF)
            low += wide
        if extras is not None:
            out_ref[:, low:] = refs[-2][...]

    ins = sum([[l, r] for l, r in pairs], [])
    rest = [extras] if extras is not None else []
    return call(
        kernel,
        (1,),
        whole_specs(ins + rest),
        fixed((tall, wide_all)),
        shape((tall, wide_all)),
        prefetch=(half,),
        after=after,
        cost=2.8, vmem=8,
    )(*near(*ins), *rest)


def keep_outer(half, spot, pairs, arrived, zs, extras=None, after=()):
    columns = [r.shape[1] // 2 for _, r in pairs]
    tall = pairs[0][0].shape[1]
    wide = sum(columns) + (TFREQ if extras is not None else 0)
    each = tall // (zs * XS * 2)
    low_zs = zs // 2
    count = len(pairs)

    def kernel(half_ref, spot_ref, *refs):
        ins, refs = refs[: 2 * count], refs[2 * count :]
        arrived_ref, refs = refs[0], refs[1:]
        if extras is not None:
            more_ref, refs = refs[0], refs[1:]
        outs, value_ref, sems = refs[:5], refs[5], refs[6]
        x0, y0 = spot_ref[1], spot_ref[2]

        def put(value, low, high):
            value_ref[..., low:high] = value.astype(HALF).reshape(zs, XS, 2, each, high - low)

        low = 0
        for n, high in enumerate(columns):
            high += low
            right = half_of(ins[2 * n + 1], half_ref[0])
            put(dot(ins[2 * n][...], right, (0, 0)) + arrived_ref[:, low:high].astype(WIDE), low, high)
            low = high
        if extras is not None:
            put(more_ref[...].astype(WIDE) + arrived_ref[:, low:].astype(WIDE), low, low + TFREQ)
        own, by_x, by_y, x_later, y_later = outs
        rest = zs - low_zs
        lows, highs = pl.ds(0, low_zs), pl.ds(low_zs, rest)
        x1, y1 = 1 - x0, 1 - y0
        moves = [
            ((pl.ds(0, zs), x0, y0), own),
            ((lows, x1, y1), by_x.at[pl.ds(0, low_zs)]),
            ((lows, x1, y0), by_x.at[pl.ds(low_zs, low_zs)]),
            ((highs, x1, y1), by_y.at[pl.ds(0, rest)]),
            ((highs, x0, y1), by_y.at[pl.ds(rest, rest)]),
            ((highs, x1, y0), x_later),
            ((lows, x0, y1), y_later),
        ]
        load([pltpu.make_async_copy(value_ref.at[cut], o, sems.at[n]) for n, (cut, o) in enumerate(moves)])

    ins = sum([[l, r] for l, r in pairs], [])
    rest = [arrived] + ([extras] if extras is not None else [])
    sizes = [(k, each, wide) for k in (zs, 2 * low_zs, 2 * (zs - low_zs), zs - low_zs, low_zs)]
    return call(
        kernel,
        (1,),
        whole_specs(ins + rest),
        [ANYWHERE] * len(sizes),
        [shape(s) for s in sizes],
        [pltpu.VMEM((zs, XS, 2, each, wide), HALF), pltpu.SemaphoreType.DMA((7,))],
        prefetch=(half, spot),
        after=after,
        token=True,
        cost=4.3, vmem=14,
    )(*near(*ins), *rest)


def plain_outer(left, right):
    return dot(left, right, (0, 0)).astype(HALF)


class Routes:
    def __init__(self, shards, reps):
        self.shards, self.reps, self.zs = shards, reps, shards // XS

    def core(self, value):
        return lax.ppermute(value, "rep", [(r, r ^ 1) for r in range(self.reps)])

    def y(self, value):
        return lax.ppermute(value, "rep", [(r, r ^ 2) for r in range(self.reps)])

    def x(self, value):
        return lax.ppermute(value, "fsdp", [(f, f ^ 1) for f in range(self.shards)])

    def shift(self, value, step):
        return lax.ppermute(value, "fsdp", [(f, (f + step * XS) % self.shards) for f in range(self.shards)])

    def z(self, value):
        lines = [[z * XS + x for z in range(self.zs)] for x in range(XS)]
        return lax.all_to_all(value, "fsdp", 0, 0, axis_index_groups=lines, tiled=True)


def z(self, value, step):
        return lax.ppermute(
            value, "fsdp", [(f, (f + step * XS) % self.shards) for f in range(self.shards)]
        )


def prepare(spot, qkv, time, small, up, out, down, zs):
    cut, part = qkv.shape[0] // 2, qkv.shape[0]
    tall = down.shape[0] // 2
    third = down.shape[1] // 2
    halves = [v.shape[1] // 2 for v in (qkv, up, out)]
    widths = [halves[0] + TFREQ, halves[1] + halves[2], tall // cut * third]
    n = len(small)

    def kernel(spot_ref, qkv_ref, time_ref, up_ref, out_ref, down_ref, *refs):
        vecs, outs, table_ref, kept, sem = refs[:n], refs[n : n + 3], refs[n + 3], refs[n + 4 : -1], refs[-1]
        load([pltpu.make_async_copy(v, h, sem.at[i]) for i, (v, h) in enumerate(zip(vecs, kept))])
        table_ref[...] = jnp.zeros_like(table_ref)
        top = 0
        for ref in kept:
            value = ref[...].astype(WIDE).reshape(1, ref.shape[0])
            for m in range(ref.shape[0] // part):
                table_ref[top : top + 1, :part] = value[:, m * part : (m + 1) * part]
                top += 1
        table = jnp.where(spot_ref[2] == 0, table_ref[...], 0.0).astype(HALF)
        first = [qkv_ref[...], jnp.where(spot_ref[3] == 0, time_ref[...], table)]
        third_parts = [down_ref[i * cut : (i + 1) * cut, :] for i in range(tall // cut)]
        for ref, parts in zip(outs, (first, [up_ref[...], out_ref[...]], third_parts)):
            here = 0
            for value in parts:
                there = slice(here, here + value.shape[1])
                if len(ref.shape) == 2:
                    ref[:, there] = value
                else:
                    for k in range(zs):
                        ref[k, :, there] = value
                here += value.shape[1]

    quarter = lambda rows, columns: pl.BlockSpec((rows, columns), lambda i, spot: (spot[2], spot[3]))
    sizes = [(zs, cut, w) if at_once else (cut, w) for w, at_once in zip(widths, (False, False, False))]
    return call(
        kernel,
        (1,),
        [
            quarter(cut, halves[0]),
            pl.BlockSpec((cut, TFREQ), lambda i, spot: (spot[2], 0)),
            quarter(cut, halves[1]),
            quarter(cut, halves[2]),
            quarter(tall, third),
        ]
        + [ANYWHERE] * n,
        [fixed(s) for s in sizes],
        [shape(s) for s in sizes],
        [pltpu.VMEM((cut, TFREQ), WIDE)]
        + [pltpu.VMEM(v.shape, HALF) for v in small]
        + [pltpu.SemaphoreType.DMA((n,))],
        prefetch=(spot,),
        cost=0.1875, vmem=6,
    )(*far(qkv, time, up, out, down, *small))


def weave(spot, zs, arrays, outs, after=()):
    arrays = list(arrays)

    def kernel(spot_ref, *refs):
        for ref, (copies, parts) in zip(refs[len(arrays) :], outs):
            here = 0
            for n, low, count, step in parts:
                cols = slice(low, low + count)
                value = refs[n][:, cols] if step is None else refs[n][lax.rem(spot_ref[0] + (zs - step), zs), :, cols]
                there = slice(here, here + count)
                if copies is None:
                    ref[:, there] = value
                else:
                    for k in range(copies):
                        ref[k, :, there] = value
                here += count

    rows = arrays[0].shape[-2]
    sizes = [(() if c is None else (c,)) + (rows, sum(p[2] for p in parts)) for c, parts in outs]
    return call(
        kernel,
        (1,),
        [SCALARS] + whole_specs(arrays),
        [fixed(s) for s in sizes],
        [shape(s) for s in sizes],
        after=after,
        cost=0.05, vmem=8,
    )(spot, *arrays)


def cut_of(layout, low, high, dx, dy):
    out, left = [], 0
    for g, dz, count in layout:
        first, last = max(low, left), min(high, left + count)
        if first < last:
            out.append((g, dz, dx, dy, first - left, last - first))
        left += count
    return out


def middle_of(count):
    return count // 2 // 128 * 128


class Gather:
    def __init__(self, spot, owns, routes):
        self.spot, self.routes = spot, routes
        self.widths = [o.shape[-1] for o in owns]
        self.arrays, self.segments = [], [[] for _ in self.widths]
        shifts = lambda o: [o] + [routes.shift(o, step) for step in range(1, routes.zs)]
        self.by_z = [shifts(o) if o.ndim == 2 else [routes.z(o)] for o in owns]
        self.line = [None] * len(owns)

    def weave(self, arrays, outs, after=()):
        return weave(self.spot, self.routes.zs, arrays, outs, after)

    def add(self, array, parts, dc=0):
        low = 0
        for g, dz, dx, dy, column, count in parts:
            self.segments[g].append((len(self.arrays), low, count, dz, dx, dy, dc, column))
            low += count
        self.arrays.append(array)

    def both(self, array, parts):
        core = self.routes.core(array)
        self.add(array, parts)
        self.add(core, parts, 1)
        return core

    def group(self, g, dims):
        used = sorted({s[0] for s in self.segments[g]})
        segments = [(used.index(s[0]),) + s[1:] for s in self.segments[g]]
        return Gathered([self.arrays[n] for n in used], segments, dims)

    def follow(self, g, after=()):
        come, width = self.by_z[g], self.widths[g]
        if len(come) > 1:
            lines = [(step, 0, width, None) for step in range(self.routes.zs)]
        else:
            lines = [(0, 0, width, step) for step in range(self.routes.zs)]
        (line,) = self.weave(come, [(None, lines)], after)
        self.line[g] = [line, self.routes.x(line), self.routes.y(line)]
        return line

    def onward(self, g, after=()):
        whole = [(g, step, self.widths[g]) for step in range(self.routes.zs)]
        count = self.routes.zs * self.widths[g]
        cut = middle_of(count)
        x2, y2, known = self.weave(
            self.line[g],
            [
                (None, [(2, 0, cut, None)]),
                (None, [(1, cut, count - cut, None)]),
                (None, [(k, 0, count, None) for k in range(3)]),
            ],
            after,
        )
        sent = x2
        x2, y2 = self.routes.x(x2), self.routes.y(y2)
        self.both(known, sum([cut_of(whole, 0, count, dx, dy) for dx, dy in ((0, 0), (1, 0), (0, 1))], []))
        self.both(x2, cut_of(whole, 0, cut, 1, 1))
        self.both(y2, cut_of(whole, cut, count, 1, 1))
        self.passed = [x2, y2]
        return sent


def total(*terms):
    return functools.reduce(lambda a, b: a + b, [t.astype(WIDE) for t in terms]).astype(HALF)


def first_hop(kept, routes):
    own, by_x, by_y, x_later, y_later = kept[:5]
    return own, routes.x(by_x), routes.y(by_y), x_later, y_later


def second_hop(state, routes, after=()):
    own, from_x, from_y, x_later, y_later = state
    rest, low = x_later.shape[0], y_later.shape[0]

    def kernel(from_x_ref, from_y_ref, x_ref, y_ref, x_out, y_out):
        x_out[...] = total(x_ref[...], from_y_ref[:rest])
        y_out[...] = total(y_ref[...], from_x_ref[:low])

    ins = (from_x, from_y, x_later, y_later)
    outs = [shape(x_later.shape), shape(y_later.shape)]
    x_later, y_later, token = call(kernel, (1,), whole_specs(ins), whole_specs(outs), outs, after=after, cost=0.5, vmem=6, token=True)(*ins)
    return own, from_x, from_y, routes.x(x_later), routes.y(y_later), token


def line_sum(spot, state, after=()):
    state = state[:5]
    own, _, _, x_late, y_late = state
    zs, rows, columns = own.shape
    low, rest = y_late.shape[0], x_late.shape[0]

    def kernel(spot_ref, own_ref, from_x, from_y, x_late, y_late, *refs):
        outs, line_ref = refs[:-1], refs[-1]
        line_ref[:low] = total(own_ref[:low], from_x[low:], y_late[...])
        line_ref[low:] = total(own_ref[low:], x_late[...], from_y[rest:])
        for step in range(zs):
            outs[step][...] = line_ref[lax.rem(spot_ref[0] + step, zs)]

    return call(
        kernel,
        (1,),
        [SCALARS] + whole_specs(state),
        [fixed((rows, columns))] * zs,
        [shape((rows, columns))] * zs,
        [pltpu.VMEM(own.shape, HALF)],
        after=after,
        cost=0.5,
        vmem=8,
        token=True,
    )(spot, *state)


def last_hops(terms, routes, after=()):
    ins = [terms[0]] + [routes.shift(v, step) for step, v in enumerate(terms[:-1]) if step]

    def kernel(*refs):
        refs[-1][...] = total(*[r[...] for r in refs[:-1]])

    size = ins[0].shape
    mine, token = call(
        kernel, (1,), whole_specs(ins), [fixed(size)], [shape(size)], after=after, cost=0.5, vmem=4, token=True
    )(*ins)
    other = routes.y(mine)
    return [mine, routes.core(mine), other, routes.core(other)], token


def in_order(pieces, y0, c0):
    rows = [
        [jnp.where(c0 == 0, a, b), jnp.where(c0 == 0, b, a)] for a, b in (pieces[0:2], pieces[2:4])
    ]
    return [
        [jnp.where(y0 == 0, rows[y][c], rows[1 - y][c]) for c in range(2)] for y in range(2)
    ]


def finish(spot, pieces, cuts, outs, vectors=(), after=()):
    rows = pieces[0].shape[0]
    count = len(outs)

    def kernel(spot_ref, *refs):
        ins, dests, small = refs[:4], refs[4 : 4 + count], refs[4 + count :]
        grid = in_order([r[...] for r in ins], spot_ref[2], spot_ref[3])
        for y in range(2):
            for c, low, wide, out, column in cuts:
                dests[out][y * rows : (y + 1) * rows, column : column + wide] = grid[y][c][
                    :, low : low + wide
                ].astype(WIDE)
        top = 0
        if small:
            table = grid[0][1][:TALL, -TFREQ:].astype(WIDE)
        for ref in small:
            each = vectors[0]
            n = ref.shape[0] // each
            parts = [table[r : r + 1, :each] for r in range(top, top + n)]
            ref[...] = jnp.concatenate(parts, axis=1).reshape(n * each)
            top += n

    lengths = list(vectors[1]) if vectors else []
    return call(
        kernel,
        (1,),
        [SCALARS] + [fixed(v.shape) for v in pieces],
        [fixed(o) for o in outs] + [fixed((n,)) for n in lengths],
        [shape(o, WIDE) for o in outs] + [shape((n,), WIDE) for n in lengths],
        after=after,
        token=True,
        cost=1.7, vmem=12,
    )(spot, *pieces)


def pair_split(value, low):
    zero = jnp.zeros_like(value)
    return jnp.concatenate([jnp.where(low, value, zero), jnp.where(low, zero, value)], axis=0)


def time_features(timesteps):
    half = TFREQ // 2
    freqs = jnp.exp(-math.log(10000.0) * jnp.arange(half).astype(WIDE) / half)
    angles = timesteps.astype(WIDE)[:, None] * freqs[None, :]
    return jnp.concatenate([jnp.cos(angles), jnp.sin(angles)], axis=1)


def layer(
    hidden,
    cotangent,
    lengths,
    bounds,
    timesteps,
    weight_qkv,
    bias_qv,
    weight_out,
    bias_out,
    gain_mid,
    shift_mid,
    weight_up,
    bias_up,
    weight_down,
    bias_down,
    gain_last,
    shift_last,
    weight_time,
):
    shards, reps = lax.axis_size("fsdp"), lax.axis_size("rep")
    rows, width = hidden.shape
    seqs = lengths.shape[0]
    part = weight_out.shape[0]
    by_hand = reps == 4 and shards == 8 and part == 96
    rep, shard = lax.axis_index("rep"), lax.axis_index("fsdp")
    spot = jnp.stack([shard // XS, shard % XS, rep // 2, rep % 2]).astype(jnp.int32)
    small = [bias_qv, bias_out, gain_mid, shift_mid, bias_up, bias_down, gain_last, shift_last]
    feats = jnp.pad(time_features(timesteps).astype(HALF), ((0, -seqs % 8), (0, 0)))
    half, out = 3 * width // 2, width // 2
    known = None
    if by_hand:
        routes = Routes(shards, reps)
        zs = routes.zs
        owns = prepare(spot, weight_qkv, weight_time, small, weight_up, weight_out, weight_down, zs)
        gather = Gather(spot, owns, routes)
        places, cut = (zs, XS, 2), part // 2
        gather.follow(0)
        gather.onward(0, gather.by_z[1])
        sent = gather.follow(1, gather.passed)
        group1 = gather.group(0, places + (cut, 2 * gather.widths[0]))
    else:
        whole = lambda v: lax.all_gather(v, "fsdp", axis=0, tiled=True)
        qkv, up, output = whole(weight_qkv), whole(weight_up), whole(weight_out)
        blank = jnp.zeros((width, TFREQ), HALF)
        group1 = Whole(jnp.concatenate([qkv[:, :half], blank, qkv[:, half:], blank], axis=1))
        group2 = Whole(
            jnp.concatenate([up[:, : 2 * width], output[:, :out], up[:, 2 * width :], output[:, out:]], axis=1)
        )
        group3 = Whole(whole(weight_down))
        table = jnp.concatenate([whole(v).reshape(-1, width) for v in small]).astype(WIDE)
        known = (whole(weight_time), jnp.pad(table, ((0, TALL - table.shape[0]), (0, 0))))

    per_seq, flat = (rows, width, seqs), (rows, width)
    start_b, qkv, table, time, whole1 = project(
        spot, bounds, hidden, feats, group1, known, per_seq, after=[sent] if by_hand else ()
    )
    mixed, stats = attend(lengths, qkv, per_seq)
    if by_hand:
        sent = gather.follow(2, [gather.onward(1, [mixed] + gather.by_z[2])])
        group2 = gather.group(1, places + (cut, 2 * gather.widths[1]))
    normed, middle, inverse, acted, slope, whole_out, whole2 = raise_up(
        spot, bounds, hidden, feats, time, mixed, table, group2, per_seq, after=[sent] if by_hand else ()
    )
    if by_hand:
        sent = gather.onward(2, [middle])
        group3 = gather.group(2, places + (weight_down.shape[0] // 2, width))
    acted, slope = raise_rest(middle, table, whole2, acted, slope, after=[sent] if by_hand else ())
    mine, away = spot[3:], 1 - spot[3:]
    activations, back, down, up_grad, sums, sent = lower(
        spot, lengths, acted, slope, normed, cotangent, table, group3, per_seq, away
    )
    first, branch, sums = back_middle(up_grad, back, normed, inverse, table, sums, whole2, flat)
    if by_hand:
        kept3 = keep_outer(mine, spot, [(acted, down)], routes.core(sent), zs, after=[branch])
        pairs2 = [(middle, up_grad), (mixed, branch)]
        sent = outer(away, pairs2, after=[kept3[-1]])
        early, sums = back_attend(
            lengths, branch, qkv, stats, sums, whole_out, per_seq, 0, seqs // 2, after=[sent]
        )
        kept2 = keep_outer(mine, spot, pairs2, routes.core(sent), zs, after=[early])
        dproj, sums = back_attend(
            lengths, branch, qkv, stats, sums, whole_out, per_seq, seqs // 2, seqs, early, after=[kept2[-1]]
        )
        state3 = second_hop(first_hop(kept3, routes), routes, after=[dproj])
    else:
        dproj, sums = back_attend(lengths, branch, qkv, stats, sums, whole_out, per_seq, 0, seqs)
    grad_hidden, extras, *more, done = back_start(
        bounds, spot, dproj, first, feats, sums, whole1, per_seq, shards if by_hand else 0, after=[state3[-1]] if by_hand else ()
    )
    if by_hand:
        state2 = second_hop(first_hop(kept2, routes), routes, after=[done])
        sent = outer(away, [(start_b, dproj)], more[0], after=[state2[-1]])
        terms3 = line_sum(spot, state3, after=[sent])
        kept1 = keep_outer(
            mine, spot, [(start_b, dproj)], routes.core(sent), zs, extras, after=[terms3[-1]]
        )
        terms2 = line_sum(spot, state2, after=[kept1[-1]])
        sums3, token = last_hops(terms3, routes, after=[terms2[-1]])
        state1 = second_hop(first_hop(kept1, routes), routes, after=[token])
        out_down, token = finish(
            spot, sums3, [(c, 0, out, 0, c * out) for c in range(2)], [weight_down.shape], after=[state1[-1]]
        )
        terms1 = line_sum(spot, state1, after=[token])
        sums2, token = last_hops(terms2, routes, after=[terms1[-1]])
        out_up, out_out, token = finish(
            spot,
            sums2,
            [(c, 0, 2 * width, 0, c * 2 * width) for c in range(2)]
            + [(c, 2 * width, out, 1, c * out) for c in range(2)],
            [weight_up.shape, weight_out.shape],
            after=[token],
        )
        sums1, _ = last_hops(terms1, routes, after=[])
        out_qkv, out_time, *out_small, _ = finish(
            spot,
            sums1,
            [(c, 0, half, 0, c * half) for c in range(2)] + [(0, half, TFREQ, 1, 0)],
            [weight_qkv.shape, weight_time.shape],
            (part, [v.shape[0] for v in small]),
        )
    else:

        def summed(v):
            v = lax.psum_scatter(v.astype(HALF), "fsdp", scatter_dimension=0, tiled=True)
            return lax.psum(v, "rep").astype(WIDE)

        out_qkv, out_out = summed(plain_outer(start_b, dproj)), summed(plain_outer(mixed, branch))
        out_up, out_down = summed(plain_outer(middle, up_grad)), summed(plain_outer(acted, down))
        out_time = summed(extras)
        counts = [v.shape[0] * shards // width for v in small]
        tops = [sum(counts[:i]) for i in range(len(counts))]
        out_small = [summed(sums[t : t + n].reshape(-1)) for t, n in zip(tops, counts)]
    return (
        activations,
        grad_hidden,
        out_qkv,
        out_small[0],
        out_out,
        out_small[1],
        out_small[2],
        out_small[3],
        out_up,
        out_small[4],
        out_down,
        out_small[5],
        out_small[6],
        out_small[7],
        out_time,
    )


def solution(mesh):
    tokens, table, vector = P(("rep", "fsdp"), None), P("fsdp", None), P("fsdp")
    per_sequence = P(("rep", "fsdp"))
    weights = (table, vector, table, vector, vector, vector, table, vector, table, vector, vector, vector, table)
    return jax.shard_map(
        layer,
        mesh=mesh,
        in_specs=(tokens, tokens, per_sequence, per_sequence, per_sequence) + weights,
        out_specs=(tokens, tokens) + weights,
        check_vma=False,
    )
```

```python
import functools
import math

import jax
import jax.numpy as jnp
from jax import lax
from jax.experimental import pallas as pl
from jax.experimental.pallas import tpu as pltpu
from jax.sharding import PartitionSpec as P

HEADS = 12
TFREQ = 128
XS = 2
TALL = 16
WIDE = jnp.float32
HALF = jnp.bfloat16
MIB = 1024 * 1024
(BIAS_Q, BIAS_V, BIAS_OUT, GAIN_MID, SHIFT_MID, BIAS_UP, BIAS_DOWN, GAIN_LAST, SHIFT_LAST) = (0, 1, 2, 3, 4, 5, 9, 10, 11)

ANYWHERE = pl.BlockSpec(memory_space=pltpu.HBM)
SCALARS = pl.BlockSpec(memory_space=pltpu.SMEM)


def dot(left, right, axes=(1, 0)):
    return lax.dot_general(
        left, right, (((axes[0],), (axes[1],)), ((), ())), preferred_element_type=WIDE
    )


def shape(dims, dtype=HALF):
    return jax.ShapeDtypeStruct(tuple(dims), dtype)


def held(dims, dtype=HALF):
    return pltpu.VMEM(tuple(dims), dtype)


def near(*values):
    return [pltpu.with_memory_space_constraint(v, pltpu.VMEM) for v in values]


def far(*values):
    return [pltpu.with_memory_space_constraint(v, pltpu.HBM) for v in values]


def fixed(dims):
    return pl.BlockSpec(tuple(dims), lambda *_: (0,) * len(dims))


def call(
    kernel, grid, in_specs, out_specs, out_shape, scratch=(), prefetch=(), after=(), aliases=None, vmem=24, cost=1.0, token=False
):
    after = list(after)
    count, n = len(in_specs), len(after)
    if token:
        results = len(out_specs)
        out_specs = list(out_specs) + [fixed((8, 128))]
        out_shape = list(out_shape) + [shape((8, 128), WIDE)]

    def run(*refs):
        start = len(prefetch) + count
        refs = refs[:start] + refs[start + n :]
        if token:
            there = refs[start + results]
            there[...] = jnp.zeros_like(there)
            refs = refs[: start + results] + refs[start + results + 1 :]
        kernel(*refs)

    return lambda *operands: pl.pallas_call(
        run,
        grid_spec=pltpu.PrefetchScalarGridSpec(
            num_scalar_prefetch=len(prefetch),
            grid=grid,
            in_specs=in_specs + [ANYWHERE] * n,
            out_specs=out_specs,
            scratch_shapes=list(scratch),
        ),
        out_shape=out_shape,
        input_output_aliases=aliases or {},
        compiler_params=pltpu.CompilerParams(vmem_limit_bytes=vmem * MIB),
        cost_estimate=pl.CostEstimate(flops=int(cost * 4.0e9), bytes_accessed=int(cost * 4.0e6), transcendentals=0),
    )(*prefetch, *operands, *after)


def norm_parts(value):
    mean = jnp.mean(value, -1, keepdims=True)
    centered = value - mean
    inverse = lax.rsqrt(jnp.mean(centered * centered, -1, keepdims=True) + 1e-05)
    return centered * inverse, inverse


def norm_back(grad, normed, inverse):
    return inverse * (
        grad
        - jnp.mean(grad, -1, keepdims=True)
        - normed * jnp.mean(grad * normed, -1, keepdims=True)
    )


def flip(index, by):
    return 1 - index if by else index


class Gathered:
    def __init__(self, arrays, segments, dims):
        self.arrays, self.segments, self.dims = list(arrays), list(segments), tuple(dims)
        self.zs = dims[0]

    def load(self, refs, place, target, sem):
        zs, _, _, rows, columns = self.dims
        z0, x0, y0, c0 = (place[i] for i in range(4))
        wide = columns // 2
        cut = self.arrays[0].shape[0]
        for n, low, count, dz, dx, dy, dc, column in self.segments:
            z = lax.rem(z0 + (zs - dz), zs)
            while count:
                block = column // wide
                step = min(count, (block + 1) * wide - column)
                first = pl.multiple_of(flip(c0, dc) * wide + column % wide, 128)
                there = target.at[
                    z, flip(x0, dx), flip(y0, dy), pl.ds(block * cut, cut), pl.ds(first, step)
                ]
                pltpu.make_async_copy(refs[n].at[:, pl.ds(low, step)], there, sem).start()
                low, column, count = low + step, column + step, count - step
        pltpu.make_async_copy(target, target, sem).wait()


class Whole:
    def __init__(self, array):
        self.arrays, self.dims = [array], array.shape

    def load(self, refs, place, target, sem):
        copy = pltpu.make_async_copy(refs[0], target, sem)
        copy.start()
        copy.wait()


def load(copies):
    for copy in copies:
        copy.start()
    for copy in copies:
        copy.wait()


def columns_of(ref, low, high):
    value = ref[..., low:high]
    return value.reshape(-1, high - low)


def whole_specs(values):
    return [fixed(v.shape) for v in values]


def vector_map(shards):
    index = lax.broadcasted_iota(jnp.int32, (TALL * shards, 1), 0)
    shard, r = index // TALL, index % TALL
    half, quarter = shards // 2, shards // 4
    query, up = r < 2, (r >= BIAS_UP) & (r < BIAS_DOWN)
    kinds = jnp.where(query, shard // half, jnp.where(up, BIAS_UP + shard // quarter, r))
    spots = jnp.where(
        query, 2 * (shard % half) + r, jnp.where(up, 4 * (shard % quarter) + r - BIAS_UP, shard)
    )
    return kinds, spots


def kind_rows(kinds, shards):
    return (kinds == lax.broadcasted_iota(jnp.int32, (TALL * shards, TALL), 1)).astype(HALF)


def table_of(pieces, width, shards):
    kinds, spots = vector_map(shards)
    values = pieces.astype(WIDE)[:, : width // shards]
    spread = jnp.concatenate([jnp.where(spots == m, values, 0.0) for m in range(shards)], axis=1)
    return dot(kind_rows(kinds, shards), spread.astype(HALF), (0, 0))


def pieces_of(table, width, shards):
    kinds, spots = vector_map(shards)
    each = width // shards
    spread = dot(kind_rows(kinds, shards), table)
    out = jnp.zeros((TALL * shards, each), WIDE)
    for m in range(shards):
        out = jnp.where(spots == m, spread[:, m * each : (m + 1) * each], out)
    blank = jnp.zeros((TALL * shards, TFREQ - each), WIDE)
    return jnp.concatenate([out, blank], axis=1).astype(HALF)


def add_time(start_of, bounds_ref, temb, seqs, span, use):
    places = lax.broadcasted_iota(jnp.int32, (span, 1), 0)
    for s in range(seqs):
        at = slice(s * span, (s + 1) * span)
        target = jnp.where(places >= bounds_ref[s], 1.0, 0.0)
        use(at, start_of[at, :].astype(WIDE) + target * temb[s : s + 1, :])


def project(place, bounds, hidden, feats, group, known, dims, after=()):
    rows, width, seqs = dims
    span = rows // seqs
    half = 3 * width // 2
    scale = (width // HEADS) ** (-0.5)
    n = len(group.arrays)
    wide = half + TFREQ

    def kernel(place_ref, bounds_ref, hidden_ref, feats_ref, *refs):
        ins, refs = refs[:n], refs[n:]
        if known:
            time_in, vec_in = refs[:2]
            refs = refs[2:]
        start_ref, qkv_ref, vec_ref, time_ref, w_ref, sem = refs
        group.load(ins, place_ref, w_ref, sem)
        if known:
            time_ref[...], table = time_in[...], vec_in[...]
        else:
            time_ref[...] = columns_of(w_ref, half, wide)
            shards = group.zs * XS
            pieces = columns_of(w_ref, wide + half, 2 * wide).reshape(shards, width // shards, TFREQ)
            table = table_of(pieces[:, :TALL].reshape(shards * TALL, TFREQ), width, shards)
        vec_ref[...] = table
        temb = dot(feats_ref[...], time_ref[...], (1, 1))

        def use(at, start):
            start_ref[at, :] = start.astype(HALF)

        add_time(hidden_ref, bounds_ref, temb, seqs, span, use)
        start_b = start_ref[...]
        first = dot(start_b, columns_of(w_ref, 0, half))
        qkv_ref[:, :width] = ((first[:, :width] + table[BIAS_Q : BIAS_Q + 1]) * scale).astype(HALF)
        qkv_ref[:, width:half] = first[:, width:].astype(HALF)
        second = dot(start_b, columns_of(w_ref, wide, wide + half))
        rest = half - width
        qkv_ref[:, half : half + rest] = second[:, :rest].astype(HALF)
        qkv_ref[:, 2 * width :] = (second[:, rest:] + table[BIAS_V : BIAS_V + 1]).astype(HALF)

    extra = list(known) if known else []
    outs = [held((rows, width)), held((rows, 3 * width)), held((TALL, width), WIDE), held((width, TFREQ)), held(group.dims)]
    return call(
        kernel,
        (1,),
        [SCALARS, SCALARS] + whole_specs([hidden, feats]) + [ANYWHERE] * n + whole_specs(extra),
        whole_specs(outs),
        outs,
        [pltpu.SemaphoreType.DMA],
        after=after,
        cost=0.4375, vmem=6,
    )(place, bounds, hidden, feats, *far(*group.arrays), *extra)


def attend(lens, qkv, dims, after=()):
    rows, width, seqs = dims
    span = rows // seqs
    pairs = width // 128

    def kernel(lens_ref, qkv_ref, mixed_ref, stats_ref):
        lane = lax.broadcasted_iota(jnp.int32, (span, 128), 1)
        low = lane < 64

        @pl.loop(0, seqs)
        def _(s):
            at = pl.ds(pl.multiple_of(s * span, span), span)
            keep = lane < lens_ref[s]
            stats = jnp.zeros((span, 128), WIDE)
            for p in range(pairs):
                cols = lambda m: slice(m * width + p * 128, m * width + (p + 1) * 128)
                keys = pair_split(qkv_ref[at, cols(1)], low)
                values = pair_split(qkv_ref[at, cols(2)], low)
                scores = dot(qkv_ref[at, cols(0)], keys, (1, 1))
                probs = []
                for h in range(2):
                    one = jnp.where(keep, scores[:, h * span : (h + 1) * span], -1e30)
                    top = jnp.max(one, -1, keepdims=True)
                    expo = jnp.exp(one - top)
                    total = jnp.sum(expo, -1, keepdims=True)
                    probs.append((expo * (1.0 / total)).astype(HALF))
                    stats = jnp.where(lane == 2 * p + h, top + jnp.log(total), stats)
                mixed_ref[at, cols(0)] = dot(jnp.concatenate(probs, axis=1), values).astype(HALF)
            stats_ref[at, :] = stats

    outs = [held((rows, width)), held((rows, 128), WIDE)]
    return call(
        kernel,
        (1,),
        [SCALARS] + whole_specs([qkv]),
        whole_specs(outs),
        outs,
        after=after,
        cost=0.4375, vmem=4,
    )(lens, *near(qkv))


def raise_up(place, bounds, hidden, feats, time, mixed, table, group, dims, after=()):
    rows, width, seqs = dims
    span = rows // seqs
    n = len(group.arrays)
    up, out = 2 * width, width // 2
    wide = up + out

    def kernel(place_ref, bounds_ref, hidden_ref, feats_ref, time_ref, mixed_ref, vec_ref, *refs):
        ins = refs[:n]
        normed_ref, middle_ref, inverse_ref, acted_ref, slope_ref, out_ref, w_ref, branch_ref, sem = refs[n:]
        row = lambda r: vec_ref[r : r + 1, :]
        group.load(ins, place_ref, w_ref, sem)
        for h in range(2):
            out_ref[:, h * out : (h + 1) * out] = columns_of(w_ref, h * wide + up, (h + 1) * wide)
        temb = dot(feats_ref[...], time_ref[...], (1, 1))
        branch_ref[...] = dot(mixed_ref[...], out_ref[...]) + row(BIAS_OUT)

        def use(at, start):
            normed, inverse = norm_parts(start + branch_ref[at, :])
            normed_ref[at, :] = normed
            middle_ref[at, :] = (normed * row(GAIN_MID) + row(SHIFT_MID)).astype(HALF)
            inverse_ref[at, :] = jnp.broadcast_to(inverse, (span, 128))

        add_time(hidden_ref, bounds_ref, temb, seqs, span, use)
        gelu_blocks((0, 1), middle_ref, w_ref, row, acted_ref, slope_ref, width, wide)

    outs = [
        held((rows, width), WIDE),
        held((rows, width)),
        held((rows, 128), WIDE),
        held((rows, 2 * up)),
        held((rows, 2 * up)),
        held((width, width)),
        held(group.dims),
    ]
    return call(
        kernel,
        (1,),
        [SCALARS, SCALARS] + whole_specs([hidden, feats, time, mixed, table]) + [ANYWHERE] * n,
        whole_specs(outs),
        outs,
        [pltpu.VMEM((rows, width), WIDE), pltpu.SemaphoreType.DMA],
        after=after,
        cost=0.54375, vmem=10,
    )(place, bounds, hidden, feats, *near(time, mixed, table), *far(*group.arrays))


def gelu_blocks(blocks, middle_ref, w_ref, row, acted_ref, slope_ref, width, wide):
    root = math.sqrt(2 / math.pi)
    for k in blocks:
        low = (k // 2) * wide + (k % 2) * width
        cols = slice(k * width, (k + 1) * width)
        u = dot(middle_ref[...], columns_of(w_ref, low, low + width)) + row(BIAS_UP + k)
        square = u * u
        gate = 0.5 + 0.5 * jnp.tanh(u * (root + (root * 0.044715) * square))
        acted = u * gate
        acted_ref[:, cols] = acted.astype(HALF)
        slope = gate + (acted - acted * gate) * (2 * root + (6 * root * 0.044715) * square)
        slope_ref[:, cols] = slope.astype(HALF)


def raise_rest(middle, table, weight, acted, slope, after=()):
    rows, width = middle.shape
    wide = weight.shape[-1] // 2

    def kernel(middle_ref, vec_ref, w_ref, acted_in, slope_in, acted_ref, slope_ref):
        row = lambda r: vec_ref[r : r + 1, :]
        gelu_blocks((2, 3), middle_ref, w_ref, row, acted_ref, slope_ref, width, wide)

    ins = [middle, table, weight, acted, slope]
    outs = [held(acted.shape), held(slope.shape)]
    return call(
        kernel,
        (1,),
        whole_specs(ins[:3]) + [pl.BlockSpec(memory_space=pltpu.VMEM)] * 2,
        [pl.BlockSpec(memory_space=pltpu.VMEM)] * 2,
        outs,
        after=after,
        aliases={3: 0, 4: 1},
        cost=0.23125, vmem=10,
    )(*near(*ins))


def lower(place, lens, acted, slope, normed, cotangent, table, group, dims, away, after=()):
    rows, width, seqs = dims
    span = rows // seqs
    n = len(group.arrays)
    tall = 4 * width

    def kernel(place_ref, lens_ref, away_ref, acted_ref, slope_ref, normed_ref, cot_ref, vec_ref, *refs):
        ins = refs[:n]
        act_ref, back_ref, down_ref, up_ref, sums_ref, sent_ref, w_ref, sem = refs[n:]
        sums_ref[...] = jnp.zeros_like(sums_ref)
        group.load(ins, place_ref, w_ref, sem)
        row = lambda r: vec_ref[r : r + 1, :]

        def count(r, value):
            sums_ref[r : r + 1, :] += jnp.sum(value, 0, keepdims=True)

        back_ref[...] = dot(acted_ref[...], columns_of(w_ref, 0, width)) + row(BIAS_DOWN)
        places = lax.broadcasted_iota(jnp.int32, (span, 1), 0)
        for s in range(seqs):
            at = slice(s * span, (s + 1) * span)
            valid = jnp.where(places < lens_ref[s], 1.0, 0.0)
            middle = normed_ref[at, :] * row(GAIN_MID) + row(SHIFT_MID)
            last, inverse = norm_parts(middle + back_ref[at, :])
            act_ref[at, :] = ((last * row(GAIN_LAST) + row(SHIFT_LAST)) * valid).astype(HALF)
            grad = cot_ref[at, :].astype(WIDE) * valid
            count(GAIN_LAST, grad * last)
            count(SHIFT_LAST, grad)
            back = norm_back(grad * row(GAIN_LAST), last, inverse)
            back_ref[at, :] = back
            down = back.astype(HALF)
            down_ref[at, :] = down
            count(BIAS_DOWN, down.astype(WIDE))
        wide = width // 2
        half = down_ref[:, pl.ds(pl.multiple_of(away_ref[0] * wide, 128), wide)]
        for k in range(4):
            cols = slice(k * width, (k + 1) * width)
            sent_ref[cols, :] = dot(acted_ref[:, cols], half, (0, 0)).astype(HALF)
        weight = columns_of(w_ref, 0, width)
        for k in range(4):
            cols = slice(k * width, (k + 1) * width)
            grad = dot(down_ref[...], weight[cols, :], (1, 1))
            up = (grad * slope_ref[:, cols].astype(WIDE)).astype(HALF)
            up_ref[:, cols] = up
            count(BIAS_UP + k, up.astype(WIDE))

    outs = [
        shape((rows, width)),
        held((rows, width), WIDE),
        held((rows, width)),
        held((rows, tall)),
        held((TALL, width), WIDE),
        shape((tall, width // 2)),
    ]
    return call(
        kernel,
        (1,),
        [SCALARS] * 3 + whole_specs([acted, slope, normed, cotangent, table]) + [ANYWHERE] * n,
        whole_specs(outs),
        outs,
        [pltpu.VMEM(group.dims, HALF), pltpu.SemaphoreType.DMA],
        after=after,
        cost=17.7, vmem=18,
    )(place, lens, away, *near(acted, slope, normed), cotangent, *near(table), *far(*group.arrays))


def back_middle(up_grad, back, normed, inverse, table, sums, weight, dims, after=()):
    rows, width = dims
    up = 2 * width
    wide = up + width // 2
    span = 128

    def kernel(up_ref, back_ref, normed_ref, inverse_ref, vec_ref, before_ref, w_ref, first_ref, branch_ref, sums_ref):
        sums_ref[...] = before_ref[...]
        first_ref[...] = dot(up_ref[:, :up], columns_of(w_ref, 0, up), (1, 1))
        first_ref[...] += dot(up_ref[:, up:], columns_of(w_ref, wide, wide + up), (1, 1))
        gain = vec_ref[GAIN_MID : GAIN_MID + 1, :]
        for s in range(rows // span):
            at = slice(s * span, (s + 1) * span)
            grad = back_ref[at, :] + first_ref[at, :]
            normed = normed_ref[at, :]
            sums_ref[GAIN_MID : GAIN_MID + 1, :] += jnp.sum(grad * normed, 0, keepdims=True)
            sums_ref[SHIFT_MID : SHIFT_MID + 1, :] += jnp.sum(grad, 0, keepdims=True)
            first = norm_back(grad * gain, normed, inverse_ref[at, :1])
            first_ref[at, :] = first
            branch = first.astype(HALF)
            branch_ref[at, :] = branch
            sums_ref[BIAS_OUT : BIAS_OUT + 1, :] += jnp.sum(branch.astype(WIDE), 0, keepdims=True)

    outs = [held((rows, width), WIDE), held((rows, width)), held((TALL, width), WIDE)]
    ins = [up_grad, back, normed, inverse, table, sums, weight]
    return call(
        kernel,
        (1,),
        whole_specs(ins),
        whole_specs(outs),
        outs,
        after=after,
        cost=5.1, vmem=8,
    )(*near(*ins))


def back_attend(lens, branch, qkv, stats, sums, weight, dims, low_seq, high_seq, earlier=None, after=()):
    rows, width, seqs = dims
    span = rows // seqs
    pairs = width // 128
    scale = (width // HEADS) ** (-0.5)
    count = high_seq - low_seq
    top = low_seq * span if earlier is not None else 0
    size = (top + count * span, 3 * width)

    def kernel(lens_ref, branch_ref, qkv_ref, stats_ref, before_ref, w_ref, *refs):
        out_ref, sums_ref, mix_ref = refs[-3:]
        sums_ref[...] = before_ref[...]
        if top:
            out_ref[:top, :] = refs[0][...]
        mix_ref[...] = dot(branch_ref[low_seq * span : high_seq * span, :], w_ref[...], (1, 1)).astype(HALF)
        lane = lax.broadcasted_iota(jnp.int32, (span, 128), 1)
        low = lane < 64

        @pl.loop(0, count)
        def _(s):
            here = pl.ds(pl.multiple_of(s * span, span), span)
            at = pl.ds(pl.multiple_of((s + low_seq) * span, span), span)
            there = pl.ds(pl.multiple_of(s * span + top, span), span)
            keep = lane < lens_ref[s + low_seq]
            for p in range(pairs):
                cols = lambda m: slice(m * width + p * 128, m * width + (p + 1) * 128)
                query, grad = qkv_ref[at, cols(0)], mix_ref[here, cols(0)]
                keys = pair_split(qkv_ref[at, cols(1)], low)
                values = pair_split(qkv_ref[at, cols(2)], low)
                scores = dot(query, keys, (1, 1))
                grad_probs = dot(grad, values, (1, 1))
                probs, dscores = [], []
                for h in range(2):
                    half = slice(h * span, (h + 1) * span)
                    lse = stats_ref[at, 2 * p + h : 2 * p + h + 1]
                    prob = jnp.exp(jnp.where(keep, scores[:, half], -1e30) - lse)
                    product = prob * grad_probs[:, half]
                    delta = jnp.sum(product, -1, keepdims=True)
                    probs.append(prob.astype(HALF))
                    dscores.append((product - prob * delta).astype(HALF))
                probs = jnp.concatenate(probs, axis=1)
                dscores = jnp.concatenate(dscores, axis=1)
                dvalues = dot(probs, grad, (0, 0))
                dkeys = dot(dscores, query, (0, 0))
                dquery = (dot(dscores, keys).astype(HALF).astype(WIDE) * scale).astype(HALF)
                out_ref[there, cols(0)] = dquery
                sums_ref[BIAS_Q : BIAS_Q + 1, cols(0)] += jnp.sum(dquery.astype(WIDE), 0, keepdims=True)
                dkeys = jnp.where(low, dkeys[:span], dkeys[span:]).astype(HALF)
                out_ref[there, cols(1)] = dkeys
                dvalues = jnp.where(low, dvalues[:span], dvalues[span:]).astype(HALF)
                out_ref[there, cols(2)] = dvalues
                sums_ref[BIAS_V : BIAS_V + 1, cols(0)] += jnp.sum(dvalues.astype(WIDE), 0, keepdims=True)

    ins = [branch, qkv, stats, sums, weight] + ([earlier] if top else [])
    outs = [held(size), held((TALL, width), WIDE)]
    return call(
        kernel,
        (1,),
        [SCALARS] + whole_specs(ins),
        whole_specs(outs),
        outs,
        [pltpu.VMEM((count * span, width), HALF)],
        after=after,
        cost=7.5, vmem=6,
    )(lens, *near(*ins))


def back_start(bounds, place, dproj, first, feats, sums, weight, dims, shards, after=()):
    rows, width, seqs = dims
    span = rows // seqs
    half = 3 * width // 2
    wide = half + TFREQ

    def kernel(bounds_ref, place_ref, dproj_ref, first_ref, feats_ref, sums_ref, w_ref, hidden_ref, *refs):
        acc_ref, temb_ref = refs[-2:]
        more_ref = refs[0]
        acc_ref[...] = dot(dproj_ref[:, :half], columns_of(w_ref, 0, half), (1, 1))
        acc_ref[...] += dot(dproj_ref[:, half:], columns_of(w_ref, wide, wide + half), (1, 1))
        temb_ref[...] = jnp.zeros_like(temb_ref)
        places = lax.broadcasted_iota(jnp.int32, (span, 1), 0)
        for s in range(seqs):
            at = slice(s * span, (s + 1) * span)
            grad = acc_ref[at, :] + first_ref[at, :]
            hidden_ref[at, :] = grad.astype(HALF)
            target = jnp.where(places >= bounds_ref[s], 1.0, 0.0)
            temb_ref[s : s + 1, :] = jnp.sum(grad * target, 0, keepdims=True)
        grad = lax.dot_general(
            temb_ref[...],
            feats_ref[...].astype(WIDE),
            (((0,), (0,)), ((), ())),
            precision=lax.Precision.HIGHEST,
            preferred_element_type=WIDE,
        )
        if not shards:
            more_ref[...] = grad
            return
        grad = grad.astype(HALF)
        pieces = pieces_of(sums_ref[...].astype(HALF), width, shards).reshape(shards, TALL, TFREQ)
        rest = jnp.zeros((shards, width // shards - TALL, TFREQ), HALF)
        pieces = jnp.concatenate([pieces, rest], axis=1).reshape(width, TFREQ)
        first_half = place_ref[3] == 0
        more_ref[...] = jnp.where(first_half, grad, pieces)
        refs[1][...] = jnp.where(first_half, pieces, grad)

    outs = [shape((rows, width))]
    outs += [held((width, TFREQ)), shape((width, TFREQ))] if shards else [shape((width, TFREQ), WIDE)]
    ins = [dproj, first, feats, sums, weight]
    return call(
        kernel,
        (1,),
        [SCALARS, SCALARS] + whole_specs(ins),
        whole_specs(outs),
        outs,
        [pltpu.VMEM((rows, width), WIDE), pltpu.VMEM(feats.shape[:1] + (width,), WIDE)],
        after=after,
        token=True,
        cost=5.7, vmem=8,
    )(bounds, place, *near(dproj, first), feats, *near(sums, weight))


def half_of(ref, half):
    wide = ref.shape[1] // 2
    return ref[:, pl.ds(pl.multiple_of(half * wide, 128), wide)]


def outer(half, pairs, extras=None, after=()):
    columns = [r.shape[1] // 2 for _, r in pairs]
    tall = pairs[0][0].shape[1]
    wide_all = sum(columns) + (TFREQ if extras is not None else 0)

    def kernel(half_ref, *refs):
        out_ref, low = refs[-1], 0
        for n, wide in enumerate(columns):
            right = half_of(refs[2 * n + 1], half_ref[0])
            out_ref[:, low : low + wide] = dot(refs[2 * n][...], right, (0, 0)).astype(HALF)
            low += wide
        if extras is not None:
            out_ref[:, low:] = refs[-2][...]

    ins = sum([[l, r] for l, r in pairs], [])
    rest = [extras] if extras is not None else []
    return call(
        kernel,
        (1,),
        whole_specs(ins + rest),
        fixed((tall, wide_all)),
        shape((tall, wide_all)),
        prefetch=(half,),
        after=after,
        cost=2.8, vmem=8,
    )(*near(*ins), *rest)


def keep_outer(half, spot, pairs, arrived, zs, extras=None, after=()):
    columns = [r.shape[1] // 2 for _, r in pairs]
    tall = pairs[0][0].shape[1]
    wide = sum(columns) + (TFREQ if extras is not None else 0)
    each = tall // (zs * XS * 2)
    low_zs = zs // 2
    count = len(pairs)

    def kernel(half_ref, spot_ref, *refs):
        ins, refs = refs[: 2 * count], refs[2 * count :]
        arrived_ref, refs = refs[0], refs[1:]
        if extras is not None:
            more_ref, refs = refs[0], refs[1:]
        outs, value_ref, sems = refs[:5], refs[5], refs[6]
        x0, y0 = spot_ref[1], spot_ref[2]

        def put(value, low, high):
            value_ref[..., low:high] = value.astype(HALF).reshape(zs, XS, 2, each, high - low)

        low = 0
        for n, high in enumerate(columns):
            high += low
            right = half_of(ins[2 * n + 1], half_ref[0])
            put(dot(ins[2 * n][...], right, (0, 0)) + arrived_ref[:, low:high].astype(WIDE), low, high)
            low = high
        if extras is not None:
            put(more_ref[...].astype(WIDE) + arrived_ref[:, low:].astype(WIDE), low, low + TFREQ)
        own, by_x, by_y, x_later, y_later = outs
        rest = zs - low_zs
        lows, highs = pl.ds(0, low_zs), pl.ds(low_zs, rest)
        x1, y1 = 1 - x0, 1 - y0
        moves = [
            ((pl.ds(0, zs), x0, y0), own),
            ((lows, x1, y1), by_x.at[pl.ds(0, low_zs)]),
            ((lows, x1, y0), by_x.at[pl.ds(low_zs, low_zs)]),
            ((highs, x1, y1), by_y.at[pl.ds(0, rest)]),
            ((highs, x0, y1), by_y.at[pl.ds(rest, rest)]),
            ((highs, x1, y0), x_later),
            ((lows, x0, y1), y_later),
        ]
        load([pltpu.make_async_copy(value_ref.at[cut], o, sems.at[n]) for n, (cut, o) in enumerate(moves)])

    ins = sum([[l, r] for l, r in pairs], [])
    rest = [arrived] + ([extras] if extras is not None else [])
    sizes = [(k, each, wide) for k in (zs, 2 * low_zs, 2 * (zs - low_zs), zs - low_zs, low_zs)]
    return call(
        kernel,
        (1,),
        whole_specs(ins + rest),
        [ANYWHERE] * len(sizes),
        [shape(s) for s in sizes],
        [pltpu.VMEM((zs, XS, 2, each, wide), HALF), pltpu.SemaphoreType.DMA((7,))],
        prefetch=(half, spot),
        after=after,
        token=True,
        cost=4.3, vmem=14,
    )(*near(*ins), *rest)


def plain_outer(left, right):
    return dot(left, right, (0, 0)).astype(HALF)


class Routes:
    def __init__(self, shards, reps):
        self.shards, self.reps, self.zs = shards, reps, shards // XS

    def core(self, value):
        return lax.ppermute(value, "rep", [(r, r ^ 1) for r in range(self.reps)])

    def y(self, value):
        return lax.ppermute(value, "rep", [(r, r ^ 2) for r in range(self.reps)])

    def x(self, value):
        return lax.ppermute(value, "fsdp", [(f, f ^ 1) for f in range(self.shards)])

    def shift(self, value, step):
        return lax.ppermute(value, "fsdp", [(f, (f + step * XS) % self.shards) for f in range(self.shards)])

    def z(self, value):
        lines = [[z * XS + x for z in range(self.zs)] for x in range(XS)]
        return lax.all_to_all(value, "fsdp", 0, 0, axis_index_groups=lines, tiled=True)


def z(self, value, step):
        return lax.ppermute(
            value, "fsdp", [(f, (f + step * XS) % self.shards) for f in range(self.shards)]
        )


def prepare(spot, qkv, time, small, up, out, down, zs):
    cut, part = qkv.shape[0] // 2, qkv.shape[0]
    tall = down.shape[0] // 2
    third = down.shape[1] // 2
    halves = [v.shape[1] // 2 for v in (qkv, up, out)]
    widths = [halves[0] + TFREQ, halves[1] + halves[2], tall // cut * third]
    n = len(small)

    def kernel(spot_ref, qkv_ref, time_ref, up_ref, out_ref, down_ref, *refs):
        vecs, outs, table_ref, kept, sem = refs[:n], refs[n : n + 3], refs[n + 3], refs[n + 4 : -1], refs[-1]
        load([pltpu.make_async_copy(v, h, sem.at[i]) for i, (v, h) in enumerate(zip(vecs, kept))])
        table_ref[...] = jnp.zeros_like(table_ref)
        top = 0
        for ref in kept:
            value = ref[...].astype(WIDE).reshape(1, ref.shape[0])
            for m in range(ref.shape[0] // part):
                table_ref[top : top + 1, :part] = value[:, m * part : (m + 1) * part]
                top += 1
        table = jnp.where(spot_ref[2] == 0, table_ref[...], 0.0).astype(HALF)
        first = [qkv_ref[...], jnp.where(spot_ref[3] == 0, time_ref[...], table)]
        third_parts = [down_ref[i * cut : (i + 1) * cut, :] for i in range(tall // cut)]
        for ref, parts in zip(outs, (first, [up_ref[...], out_ref[...]], third_parts)):
            here = 0
            for value in parts:
                there = slice(here, here + value.shape[1])
                if len(ref.shape) == 2:
                    ref[:, there] = value
                else:
                    for k in range(zs):
                        ref[k, :, there] = value
                here += value.shape[1]

    quarter = lambda rows, columns: pl.BlockSpec((rows, columns), lambda i, spot: (spot[2], spot[3]))
    sizes = [(zs, cut, w) if at_once else (cut, w) for w, at_once in zip(widths, (False, False, False))]
    return call(
        kernel,
        (1,),
        [
            quarter(cut, halves[0]),
            pl.BlockSpec((cut, TFREQ), lambda i, spot: (spot[2], 0)),
            quarter(cut, halves[1]),
            quarter(cut, halves[2]),
            quarter(tall, third),
        ]
        + [ANYWHERE] * n,
        [fixed(s) for s in sizes],
        [shape(s) for s in sizes],
        [pltpu.VMEM((cut, TFREQ), WIDE)]
        + [pltpu.VMEM(v.shape, HALF) for v in small]
        + [pltpu.SemaphoreType.DMA((n,))],
        prefetch=(spot,),
        cost=0.1875, vmem=6,
    )(*far(qkv, time, up, out, down, *small))


def weave(spot, zs, arrays, outs, after=()):
    arrays = list(arrays)

    def kernel(spot_ref, *refs):
        for ref, (copies, parts) in zip(refs[len(arrays) :], outs):
            here = 0
            for n, low, count, step in parts:
                cols = slice(low, low + count)
                value = refs[n][:, cols] if step is None else refs[n][lax.rem(spot_ref[0] + (zs - step), zs), :, cols]
                there = slice(here, here + count)
                if copies is None:
                    ref[:, there] = value
                else:
                    for k in range(copies):
                        ref[k, :, there] = value
                here += count

    rows = arrays[0].shape[-2]
    sizes = [(() if c is None else (c,)) + (rows, sum(p[2] for p in parts)) for c, parts in outs]
    return call(
        kernel,
        (1,),
        [SCALARS] + whole_specs(arrays),
        [fixed(s) for s in sizes],
        [shape(s) for s in sizes],
        after=after,
        cost=0.05, vmem=8,
    )(spot, *arrays)


def cut_of(layout, low, high, dx, dy):
    out, left = [], 0
    for g, dz, count in layout:
        first, last = max(low, left), min(high, left + count)
        if first < last:
            out.append((g, dz, dx, dy, first - left, last - first))
        left += count
    return out


def middle_of(count):
    return count // 2 // 128 * 128


class Gather:
    def __init__(self, spot, owns, routes):
        self.spot, self.routes = spot, routes
        self.widths = [o.shape[-1] for o in owns]
        self.arrays, self.segments = [], [[] for _ in self.widths]
        shifts = lambda o: [o] + [routes.shift(o, step) for step in range(1, routes.zs)]
        self.by_z = [shifts(o) if o.ndim == 2 else [routes.z(o)] for o in owns]
        self.line = [None] * len(owns)

    def weave(self, arrays, outs, after=()):
        return weave(self.spot, self.routes.zs, arrays, outs, after)

    def add(self, array, parts, dc=0):
        low = 0
        for g, dz, dx, dy, column, count in parts:
            self.segments[g].append((len(self.arrays), low, count, dz, dx, dy, dc, column))
            low += count
        self.arrays.append(array)

    def both(self, array, parts):
        core = self.routes.core(array)
        self.add(array, parts)
        self.add(core, parts, 1)
        return core

    def group(self, g, dims):
        used = sorted({s[0] for s in self.segments[g]})
        segments = [(used.index(s[0]),) + s[1:] for s in self.segments[g]]
        return Gathered([self.arrays[n] for n in used], segments, dims)

    def follow(self, g, after=()):
        come, width = self.by_z[g], self.widths[g]
        if len(come) > 1:
            lines = [(step, 0, width, None) for step in range(self.routes.zs)]
        else:
            lines = [(0, 0, width, step) for step in range(self.routes.zs)]
        (line,) = self.weave(come, [(None, lines)], after)
        self.line[g] = [line, self.routes.x(line), self.routes.y(line)]
        return line

    def onward(self, g, after=()):
        whole = [(g, step, self.widths[g]) for step in range(self.routes.zs)]
        count = self.routes.zs * self.widths[g]
        cut = middle_of(count)
        x2, y2, known = self.weave(
            self.line[g],
            [
                (None, [(2, 0, cut, None)]),
                (None, [(1, cut, count - cut, None)]),
                (None, [(k, 0, count, None) for k in range(3)]),
            ],
            after,
        )
        sent = x2
        x2, y2 = self.routes.x(x2), self.routes.y(y2)
        self.both(known, sum([cut_of(whole, 0, count, dx, dy) for dx, dy in ((0, 0), (1, 0), (0, 1))], []))
        self.both(x2, cut_of(whole, 0, cut, 1, 1))
        self.both(y2, cut_of(whole, cut, count, 1, 1))
        self.passed = [x2, y2]
        return sent


def total(*terms):
    return functools.reduce(lambda a, b: a + b, [t.astype(WIDE) for t in terms]).astype(HALF)


def first_hop(kept, routes):
    own, by_x, by_y, x_later, y_later = kept[:5]
    return own, routes.x(by_x), routes.y(by_y), x_later, y_later


def second_hop(state, routes, after=()):
    own, from_x, from_y, x_later, y_later = state
    rest, low = x_later.shape[0], y_later.shape[0]

    def kernel(from_x_ref, from_y_ref, x_ref, y_ref, x_out, y_out):
        x_out[...] = total(x_ref[...], from_y_ref[:rest])
        y_out[...] = total(y_ref[...], from_x_ref[:low])

    ins = (from_x, from_y, x_later, y_later)
    outs = [shape(x_later.shape), shape(y_later.shape)]
    x_later, y_later, token = call(kernel, (1,), whole_specs(ins), whole_specs(outs), outs, after=after, cost=0.5, vmem=6, token=True)(*ins)
    return own, from_x, from_y, routes.x(x_later), routes.y(y_later), token


def line_sum(spot, state, after=()):
    state = state[:5]
    own, _, _, x_late, y_late = state
    zs, rows, columns = own.shape
    low, rest = y_late.shape[0], x_late.shape[0]

    def kernel(spot_ref, own_ref, from_x, from_y, x_late, y_late, *refs):
        outs, line_ref = refs[:-1], refs[-1]
        line_ref[:low] = total(own_ref[:low], from_x[low:], y_late[...])
        line_ref[low:] = total(own_ref[low:], x_late[...], from_y[rest:])
        for step in range(zs):
            outs[step][...] = line_ref[lax.rem(spot_ref[0] + step, zs)]

    return call(
        kernel,
        (1,),
        [SCALARS] + whole_specs(state),
        [fixed((rows, columns))] * zs,
        [shape((rows, columns))] * zs,
        [pltpu.VMEM(own.shape, HALF)],
        after=after,
        cost=0.5,
        vmem=8,
        token=True,
    )(spot, *state)


def last_hops(terms, routes, after=()):
    ins = [terms[0]] + [routes.shift(v, step) for step, v in enumerate(terms[:-1]) if step]

    def kernel(*refs):
        refs[-1][...] = total(*[r[...] for r in refs[:-1]])

    size = ins[0].shape
    mine, token = call(
        kernel, (1,), whole_specs(ins), [fixed(size)], [shape(size)], after=after, cost=0.5, vmem=4, token=True
    )(*ins)
    other = routes.y(mine)
    return [mine, routes.core(mine), other, routes.core(other)], token


def in_order(pieces, y0, c0):
    rows = [
        [jnp.where(c0 == 0, a, b), jnp.where(c0 == 0, b, a)] for a, b in (pieces[0:2], pieces[2:4])
    ]
    return [
        [jnp.where(y0 == 0, rows[y][c], rows[1 - y][c]) for c in range(2)] for y in range(2)
    ]


def finish(spot, pieces, cuts, outs, vectors=(), after=()):
    rows = pieces[0].shape[0]
    count = len(outs)

    def kernel(spot_ref, *refs):
        ins, dests, small = refs[:4], refs[4 : 4 + count], refs[4 + count :]
        grid = in_order([r[...] for r in ins], spot_ref[2], spot_ref[3])
        for y in range(2):
            for c, low, wide, out, column in cuts:
                dests[out][y * rows : (y + 1) * rows, column : column + wide] = grid[y][c][
                    :, low : low + wide
                ].astype(WIDE)
        top = 0
        if small:
            table = grid[0][1][:TALL, -TFREQ:].astype(WIDE)
        for ref in small:
            each = vectors[0]
            n = ref.shape[0] // each
            parts = [table[r : r + 1, :each] for r in range(top, top + n)]
            ref[...] = jnp.concatenate(parts, axis=1).reshape(n * each)
            top += n

    lengths = list(vectors[1]) if vectors else []
    return call(
        kernel,
        (1,),
        [SCALARS] + [fixed(v.shape) for v in pieces],
        [fixed(o) for o in outs] + [fixed((n,)) for n in lengths],
        [shape(o, WIDE) for o in outs] + [shape((n,), WIDE) for n in lengths],
        after=after,
        token=True,
        cost=1.7, vmem=12,
    )(spot, *pieces)


def pair_split(value, low):
    zero = jnp.zeros_like(value)
    return jnp.concatenate([jnp.where(low, value, zero), jnp.where(low, zero, value)], axis=0)


def time_features(timesteps):
    half = TFREQ // 2
    freqs = jnp.exp(-math.log(10000.0) * jnp.arange(half).astype(WIDE) / half)
    angles = timesteps.astype(WIDE)[:, None] * freqs[None, :]
    return jnp.concatenate([jnp.cos(angles), jnp.sin(angles)], axis=1)


def layer(
    hidden,
    cotangent,
    lengths,
    bounds,
    timesteps,
    weight_qkv,
    bias_qv,
    weight_out,
    bias_out,
    gain_mid,
    shift_mid,
    weight_up,
    bias_up,
    weight_down,
    bias_down,
    gain_last,
    shift_last,
    weight_time,
):
    shards, reps = lax.axis_size("fsdp"), lax.axis_size("rep")
    rows, width = hidden.shape
    seqs = lengths.shape[0]
    part = weight_out.shape[0]
    by_hand = reps == 4 and shards == 8 and part == 96
    rep, shard = lax.axis_index("rep"), lax.axis_index("fsdp")
    spot = jnp.stack([shard // XS, shard % XS, rep // 2, rep % 2]).astype(jnp.int32)
    small = [bias_qv, bias_out, gain_mid, shift_mid, bias_up, bias_down, gain_last, shift_last]
    feats = jnp.pad(time_features(timesteps).astype(HALF), ((0, -seqs % 8), (0, 0)))
    half, out = 3 * width // 2, width // 2
    known = None
    if by_hand:
        routes = Routes(shards, reps)
        zs = routes.zs
        owns = prepare(spot, weight_qkv, weight_time, small, weight_up, weight_out, weight_down, zs)
        gather = Gather(spot, owns, routes)
        places, cut = (zs, XS, 2), part // 2
        gather.follow(0)
        gather.onward(0, gather.by_z[1])
        sent = gather.follow(1, gather.passed)
        group1 = gather.group(0, places + (cut, 2 * gather.widths[0]))
    else:
        whole = lambda v: lax.all_gather(v, "fsdp", axis=0, tiled=True)
        qkv, up, output = whole(weight_qkv), whole(weight_up), whole(weight_out)
        blank = jnp.zeros((width, TFREQ), HALF)
        group1 = Whole(jnp.concatenate([qkv[:, :half], blank, qkv[:, half:], blank], axis=1))
        group2 = Whole(
            jnp.concatenate([up[:, : 2 * width], output[:, :out], up[:, 2 * width :], output[:, out:]], axis=1)
        )
        group3 = Whole(whole(weight_down))
        table = jnp.concatenate([whole(v).reshape(-1, width) for v in small]).astype(WIDE)
        known = (whole(weight_time), jnp.pad(table, ((0, TALL - table.shape[0]), (0, 0))))

    per_seq, flat = (rows, width, seqs), (rows, width)
    start_b, qkv, table, time, whole1 = project(
        spot, bounds, hidden, feats, group1, known, per_seq, after=[sent] if by_hand else ()
    )
    mixed, stats = attend(lengths, qkv, per_seq)
    if by_hand:
        sent = gather.follow(2, [gather.onward(1, [mixed] + gather.by_z[2])])
        group2 = gather.group(1, places + (cut, 2 * gather.widths[1]))
    normed, middle, inverse, acted, slope, whole_out, whole2 = raise_up(
        spot, bounds, hidden, feats, time, mixed, table, group2, per_seq, after=[sent] if by_hand else ()
    )
    if by_hand:
        sent = gather.onward(2, [middle])
        group3 = gather.group(2, places + (weight_down.shape[0] // 2, width))
    acted, slope = raise_rest(middle, table, whole2, acted, slope, after=[sent] if by_hand else ())
    mine, away = spot[3:], 1 - spot[3:]
    activations, back, down, up_grad, sums, sent = lower(
        spot, lengths, acted, slope, normed, cotangent, table, group3, per_seq, away
    )
    first, branch, sums = back_middle(up_grad, back, normed, inverse, table, sums, whole2, flat)
    if by_hand:
        kept3 = keep_outer(mine, spot, [(acted, down)], routes.core(sent), zs, after=[branch])
        pairs2 = [(middle, up_grad), (mixed, branch)]
        sent = outer(away, pairs2, after=[kept3[-1]])
        early, sums = back_attend(
            lengths, branch, qkv, stats, sums, whole_out, per_seq, 0, seqs // 2, after=[sent]
        )
        kept2 = keep_outer(mine, spot, pairs2, routes.core(sent), zs, after=[early])
        dproj, sums = back_attend(
            lengths, branch, qkv, stats, sums, whole_out, per_seq, seqs // 2, seqs, early, after=[kept2[-1]]
        )
        state3 = second_hop(first_hop(kept3, routes), routes, after=[dproj])
    else:
        dproj, sums = back_attend(lengths, branch, qkv, stats, sums, whole_out, per_seq, 0, seqs)
    grad_hidden, extras, *more, done = back_start(
        bounds, spot, dproj, first, feats, sums, whole1, per_seq, shards if by_hand else 0, after=[state3[-1]] if by_hand else ()
    )
    if by_hand:
        state2 = second_hop(first_hop(kept2, routes), routes, after=[done])
        sent = outer(away, [(start_b, dproj)], more[0], after=[state2[-1]])
        kept1 = keep_outer(mine, spot, [(start_b, dproj)], routes.core(sent), zs, extras, after=[state2[-1]])
        terms3 = line_sum(spot, state3, after=[kept1[-1]])
        terms2 = line_sum(spot, state2, after=[terms3[-1]])
        sums3, token = last_hops(terms3, routes, after=[terms2[-1]])
        state1 = second_hop(first_hop(kept1, routes), routes, after=[token])
        out_down, token = finish(
            spot, sums3, [(c, 0, out, 0, c * out) for c in range(2)], [weight_down.shape], after=[state1[-1]]
        )
        terms1 = line_sum(spot, state1, after=[token])
        sums2, token = last_hops(terms2, routes, after=[terms1[-1]])
        out_up, out_out, token = finish(
            spot,
            sums2,
            [(c, 0, 2 * width, 0, c * 2 * width) for c in range(2)]
            + [(c, 2 * width, out, 1, c * out) for c in range(2)],
            [weight_up.shape, weight_out.shape],
            after=[token],
        )
        sums1, _ = last_hops(terms1, routes, after=[])
        out_qkv, out_time, *out_small, _ = finish(
            spot,
            sums1,
            [(c, 0, half, 0, c * half) for c in range(2)] + [(0, half, TFREQ, 1, 0)],
            [weight_qkv.shape, weight_time.shape],
            (part, [v.shape[0] for v in small]),
            after=[token],
        )
    else:

        def summed(v):
            v = lax.psum_scatter(v.astype(HALF), "fsdp", scatter_dimension=0, tiled=True)
            return lax.psum(v, "rep").astype(WIDE)

        out_qkv, out_out = summed(plain_outer(start_b, dproj)), summed(plain_outer(mixed, branch))
        out_up, out_down = summed(plain_outer(middle, up_grad)), summed(plain_outer(acted, down))
        out_time = summed(extras)
        counts = [v.shape[0] * shards // width for v in small]
        tops = [sum(counts[:i]) for i in range(len(counts))]
        out_small = [summed(sums[t : t + n].reshape(-1)) for t, n in zip(tops, counts)]
    return (
        activations,
        grad_hidden,
        out_qkv,
        out_small[0],
        out_out,
        out_small[1],
        out_small[2],
        out_small[3],
        out_up,
        out_small[4],
        out_down,
        out_small[5],
        out_small[6],
        out_small[7],
        out_time,
    )


def solution(mesh):
    tokens, table, vector = P(("rep", "fsdp"), None), P("fsdp", None), P("fsdp")
    per_sequence = P(("rep", "fsdp"))
    weights = (table, vector, table, vector, vector, vector, table, vector, table, vector, vector, vector, table)
    return jax.shard_map(
        layer,
        mesh=mesh,
        in_specs=(tokens, tokens, per_sequence, per_sequence, per_sequence) + weights,
        out_specs=(tokens, tokens) + weights,
        check_vma=False,
    )
```
